256 devices in a mesh: ctx: 64 (over x, z, y_lo), head: 4 (over y_hi, core).
Axes of the slice: x: 4, y: 4 (y_hi: 2, y_lo: 2; y = y_hi * 2 + y_lo), z: 8, core: 2. Of those that a mesh axis runs over, the one named last changes fastest.
Arguments:
- queries: bfloat16 [24576, 8192], P('ctx', 'head'), may hold values from -160 to 160
- keys: bfloat16 [24576, 1024], P('ctx', 'head'), may hold values from -4 to 4
- values: bfloat16 [24576, 1024], P('ctx', 'head'), may hold values from -6 to 6
- keep_rows: int32 [64, 8, 64, 4], P('ctx', 'head'), may hold values from 0 to 383
- keep_dest: int32 [64, 8, 64], P('ctx', 'head'), may hold values from 0 to 63, as said below
- keep_count: int32 [64, 8, 64], P('ctx', 'head'), may hold values from 1 to 4, as said below
Outputs:
- attended: bfloat16 [24576, 8192], P('ctx', 'head')
- key_scores: float32 [24576], P('ctx')
- decode_cache: bfloat16 [64, 64, 4, 8, 256], P('ctx', None, None, 'head')
The draws below stay inside these ranges and needn't reach their ends.
Inputs may be any that keep to these rules, and one draw needn't show every extreme that they name: For each source shard and head, keep_dest over j is a permutation of 0 to 63. `keep_count`: in every draw some decode shard receives 4 live slots in every block.
All inputs are finite; a program needn't handle non-finite values.
Results may differ from the reference program's by a relative error of at most 0.0045.
Values may be sent and summed in bfloat16 or wider, within the bound.
A program may use at most 64 MiB of HBM per device.

```python
import jax
import jax.numpy as jnp
from jax import lax

HD = 128
KVH = 8
QPK = 8
BLK = 192
KB = 4
QH = 64
TOK_DEV = 384
TOKENS = 24576
N_CTX = 64


def shared_keys(key):
    key = jax.random.fold_in(key, 101)
    return jnp.clip(jax.random.normal(key, (TOKENS, KVH * HD), jnp.float32), -4.0, 4.0)


def destinations(key):
    key = jax.random.fold_in(key, 202)
    bits = jax.random.randint(key, (N_CTX, KVH, N_CTX), 0, 1 << 20)
    ranked = bits * N_CTX + jnp.arange(N_CTX, dtype=jnp.int32)
    return jnp.argsort(ranked, axis=-1).astype(jnp.int32)


def draw_keys(key, part):
    return shared_keys(key).astype(jnp.bfloat16)


def draw_queries(key, part):
    key = jax.random.fold_in(key, 11)
    found = jnp.clip(jax.random.normal(key, (TOKENS, QH * HD), jnp.float32), -6.0, 6.0)
    return found.astype(jnp.bfloat16)


def draw_keep_dest(key, part):
    return destinations(key)


def draw_keep_count(key, part):
    dest = destinations(key)
    key = jax.random.fold_in(key, 5)
    first, second = jax.random.split(key)
    counts = jax.random.randint(first, (N_CTX, KVH, N_CTX), 1, KB + 1)
    chosen = jax.random.randint(second, (), 0, N_CTX)
    return jnp.where(dest == chosen, KB, counts).astype(jnp.int32)


def place_ends(entries, stream_key, low, top_value):
    place = [jax.random.randint(jax.random.fold_in(stream_key, axis), (), 0, length) for axis, length in enumerate(entries.shape)]
    longest = entries.shape.index(max(entries.shape))
    next_to = place[:longest] + [(place[longest] + 1) % entries.shape[longest]] + place[longest + 1:]
    return entries.at[tuple(place)].set(low).at[tuple(next_to)].set(top_value)


def shard_levels(stream_key, shape, cuts, low, top_value):
    def one(axis_at, shards_of):
        steps = jax.random.uniform(jax.random.fold_in(jax.random.fold_in(stream_key, 6), axis_at), (shards_of,), jnp.float32, low / len(cuts), top_value / len(cuts))
        return jnp.repeat(jnp.exp(steps), shape[axis_at] // shards_of).reshape((-1,) + (1,) * (len(shape) - axis_at - 1))

    gain = one(*cuts[0])
    for cut in cuts[1:]:
        gain = gain * one(*cut)
    return gain


def bell_draw(own_key, shape, width, most, cuts=(), held_as=jnp.bfloat16):
    drawn = width * jax.random.normal(own_key, shape, jnp.float32)
    if cuts:
        drawn = drawn * shard_levels(own_key, shape, cuts, -0.22, 0.18)
    return jnp.clip(drawn, -most, most).astype(held_as)


def setup_inputs(seed: int = 0) -> dict:
    key_of = jax.random.split(jax.random.key(seed), 7)
    queries = draw_queries(jax.random.fold_in(key_of[6], 71), 0)
    keys = draw_keys(jax.random.fold_in(key_of[6], 71), 0)
    values = bell_draw(key_of[2], (TOKENS, KVH * HD), 1.0, 6.0, ((0, 64), (1, 4)))
    keep_rows = place_ends(jax.random.randint(key_of[3], (N_CTX, KVH, N_CTX, KB), 0, TOK_DEV), jax.random.fold_in(key_of[3], 1), 0, TOK_DEV - 1).astype(jnp.int32)
    keep_dest = draw_keep_dest(jax.random.fold_in(key_of[6], 71), 0)
    keep_count = draw_keep_count(jax.random.fold_in(key_of[6], 71), 0)
    return dict(queries=queries, keys=keys, values=values, keep_rows=keep_rows, keep_dest=keep_dest, keep_count=keep_count)


def block_positions(shard, half):
    index = jnp.arange(2 * half, dtype=jnp.int32)
    return jnp.where(index < half, shard * half + index, (2 * N_CTX - 1 - shard) * half + index - half).astype(jnp.int32)


def reference(queries, keys, values, keep_rows, keep_dest, keep_count):
    tok = 2 * BLK
    scale = HD ** -0.5
    q_shards = queries.reshape(N_CTX, tok, KVH, QPK, HD)
    k_shards = keys.reshape(N_CTX, tok, KVH, HD)
    v_shards = values.reshape(N_CTX, tok, KVH, HD)

    def one_shard(shard):
        sources = [((shard - step) % N_CTX).astype(jnp.int32) for step in range(3)]
        key_cat = jnp.concatenate([lax.dynamic_index_in_dim(k_shards, s, 0, keepdims=False) for s in sources], 0).astype(jnp.float32)
        val_cat = jnp.concatenate([lax.dynamic_index_in_dim(v_shards, s, 0, keepdims=False) for s in sources], 0).astype(jnp.float32)
        key_pos = jnp.concatenate([block_positions(s, BLK) for s in sources])
        query_pos = block_positions(shard, BLK)
        query_blk = lax.dynamic_index_in_dim(q_shards, shard, 0, keepdims=False).astype(jnp.float32)
        score = jnp.einsum('qgrd,kgd->grqk', query_blk, key_cat) * scale
        score = jnp.where((key_pos[None, :] <= query_pos[:, None])[None, None], score, -jnp.inf)
        top = jnp.max(score, -1, keepdims=True)
        weight = jnp.exp(score - top)
        total = jnp.sum(weight, -1, keepdims=True)
        rounded = lax.optimization_barrier(weight.astype(jnp.bfloat16)).astype(jnp.float32)
        product = jnp.einsum('grqk,kgd->grqd', rounded, val_cat) / total
        output = jnp.transpose(product, (2, 0, 1, 3)).reshape(tok, KVH * QPK * HD).astype(jnp.bfloat16)
        column = jnp.sum(weight / total, axis=(0, 1, 2)) / QH
        return output, column.reshape(3, tok)

    outputs, columns = lax.map(one_shard, jnp.arange(N_CTX, dtype=jnp.int32))
    attended = outputs.reshape(N_CTX * tok, KVH * QPK * HD)
    key_scores = columns[:, 0] + jnp.roll(columns[:, 1], -1, 0) + jnp.roll(columns[:, 2], -2, 0)
    key_scores = key_scores.reshape(N_CTX * tok)

    pairs = jnp.concatenate([k_shards, v_shards], axis=3)
    head_index = jnp.arange(KVH, dtype=jnp.int32)
    block_index = jnp.arange(N_CTX, dtype=jnp.int32)

    def one_source(shard):
        local = lax.dynamic_index_in_dim(pairs, shard, 0, keepdims=False)
        rows = lax.dynamic_index_in_dim(keep_rows, shard, 0, keepdims=False)
        dest = lax.dynamic_index_in_dim(keep_dest, shard, 0, keepdims=False)
        live = lax.dynamic_index_in_dim(keep_count, shard, 0, keepdims=False)
        picked = local[rows, head_index[:, None, None]]
        slot = jnp.arange(KB, dtype=jnp.int32)
        picked = jnp.where((slot[None, None, :] < live[:, :, None])[..., None], picked, jnp.zeros((), jnp.bfloat16))
        match = dest[:, :, None] == block_index[None, None, :]
        inverse = jnp.sum(block_index[None, :, None] * match, axis=1).astype(jnp.int32)
        return picked[head_index[:, None], inverse]

    sent = lax.map(one_source, jnp.arange(N_CTX, dtype=jnp.int32))
    decode_cache = jnp.transpose(sent, (2, 0, 3, 1, 4))
    return attended, key_scores, decode_cache
```

```python
import jax
import jax.numpy as jnp
from jax import lax
from jax.experimental import pallas as pl
from jax.experimental.pallas import tpu as pltpu
from jax.sharding import PartitionSpec as P

HD = 128
KB = 4
QH = 64
TOK = 384
HALF = 192
G = 2
QPK = 8
HEADS = G * QPK
N_CTX = 64
F32 = jnp.float32
BF = jnp.bfloat16
LOG2E_SCALE = HD**-0.5 * 1.4426950408889634
MESH = pl.DeviceIdType.MESH


def dot(a, b):
    return lax.dot_general(a, b, (((1,), (0,)), ((), ())), preferred_element_type=F32)


def dot_t(a, b):
    return lax.dot_general(a, b, (((1,), (1,)), ((), ())), preferred_element_type=F32)


def iota(shape, dim):
    return lax.broadcasted_iota(jnp.int32, shape, dim)


def with_ones(v):
    return jnp.concatenate([v, jnp.ones(v.shape, BF)], 1)


def column_sum(w, f):
    r, n = w.shape
    return jnp.sum((w.astype(F32) * f[:, :1]).reshape(r // 8, 8, n), 0)


def emit(units, skew):
    stages = max(len(u) for u in units)
    for t in range(len(units) + (stages - 1) * skew):
        for k in range(stages):
            i = t - k * skew
            if 0 <= i < len(units) and k < len(units[i]):
                units[i][k]()


def kernel(
    q_hbm, k_hbm, v_hbm, rows_hbm, dest_hbm, count_hbm,
    out_hbm, score_hbm, cache_hbm,
    q_ref, k_ref, v_ref, rows_ref, dest_ref, count_ref,
    kn_ref, vn_ref, stage, outgoing, plane, out_ref,
    ot1, m1, wl, wh, col_own, col_near, col_send, col_recv, score_ref,
    in_sem, out_sem, kv_send, kv_recv, p1_send, p1_recv, p2_send, p2_recv, ks_send, ks_recv,
):
    c = lax.axis_index("ctx")
    hd = lax.axis_index("head")
    x = lax.div(c, 16)
    z = lax.rem(lax.div(c, 2), 8)
    y = lax.rem(c, 2)
    xy = x * 2 + y

    def ctx(delta):
        return lax.rem(c + delta + N_CTX, N_CTX)

    def xy_ctx(i):
        p = lax.rem(xy + i + 8, 8)
        return p, lax.div(p, 2) * 16 + z * 2 + lax.rem(p, 2)

    def z_ctx(i):
        p = lax.rem(z + i + 8, 8)
        return p, x * 16 + p * 2 + y

    def head_of(i):
        return lax.rem(hd + i, 4)

    loads = [
        pltpu.make_async_copy(src, dst, in_sem.at[i])
        for i, (src, dst) in enumerate(
            [
                (k_hbm, k_ref), (v_hbm, v_ref), (rows_hbm, rows_ref), (dest_hbm, dest_ref),
                (count_hbm, count_ref),
                (q_hbm.at[:, pl.ds(0, QPK * HD)], q_ref.at[:, pl.ds(0, QPK * HD)]),
                (q_hbm.at[:, pl.ds(QPK * HD, QPK * HD)], q_ref.at[:, pl.ds(QPK * HD, QPK * HD)]),
            ]
        )
    ]
    for load in loads:
        load.start()

    barrier = pltpu.get_barrier_semaphore()
    greeted = [(ctx(-1), hd), (ctx(-2), hd)]
    greeted += [(xy_ctx(i)[1], hd) for i in range(1, 8)]
    greeted += [(z_ctx(i)[1], hd) for i in range(1, 8)]
    greeted += [(ctx(1), head_of(i)) for i in range(4)]
    greeted += [(ctx(2), head_of(i)) for i in range(4)]
    greeted += [(c, head_of(i)) for i in range(1, 4)]
    for a, b in greeted:
        pl.semaphore_signal(barrier, inc=1, device_id={"ctx": a, "head": b}, device_id_type=MESH)

    for load in loads[:2]:
        load.wait()
    pl.semaphore_wait(barrier, len(greeted))

    def kv_copy(which, slot, rows, delta):
        src = (k_ref, v_ref)[which].at[pl.ds(rows, HALF)]
        dst = (kn_ref, vn_ref)[which].at[pl.ds(slot * HALF, HALF)]
        return pltpu.make_async_remote_copy(
            src_ref=src, dst_ref=dst,
            send_sem=kv_send.at[which, slot], recv_sem=kv_recv.at[which, slot],
            device_id={"ctx": ctx(delta), "head": hd}, device_id_type=MESH,
        )

    near_a = [kv_copy(w, 0, 0, 1) for w in range(2)]
    near_b = [kv_copy(w, 1, 0, 2) for w in range(2)]
    far_b = [kv_copy(w, 2, HALF, 2) for w in range(2)]
    far_a = [kv_copy(w, 3, HALF, 1) for w in range(2)]
    for w in range(2):
        near_a[w].start()
        near_b[w].start()

    @pl.when(c >= N_CTX - 2)
    def _():
        for copy in far_b:
            copy.start()

    @pl.when(c == N_CTX - 1)
    def _():
        for copy in far_a:
            copy.start()

    for load in loads[2:5]:
        load.wait()
    d = iota((N_CTX, N_CTX), 0)
    order = (d >> 4) * 16 + (d & 7) * 2 + ((d >> 3) & 1)
    lane = iota((N_CTX, TOK), 1).astype(F32)
    for g in range(G):
        match = dest_ref[0, g : g + 1, :] == order
        live = jnp.sum(
            jnp.where(match, count_ref[0, g : g + 1, :].astype(F32), 0.0), 1, keepdims=True
        )
        match = jnp.where(match, 1.0, 0.0).astype(BF)
        rows = rows_ref[0, g]
        high = dot(match, (rows >> 4).astype(F32).astype(BF))
        low = dot(match, (rows & 15).astype(F32).astype(BF))
        rows = high * 16.0 + low
        pair = jnp.concatenate(
            [k_ref[:, g * HD : (g + 1) * HD], v_ref[:, g * HD : (g + 1) * HD]], 1
        )
        for t in range(KB):
            row = jnp.where(live > t, rows[:, t : t + 1], -1.0)
            pick = jnp.where(row == lane, 1.0, 0.0).astype(BF)
            picked = dot(pick, pair)
            for half in range(2):
                stage[pl.ds(t * 4 + half * 2 + g, N_CTX, stride=16), :] = picked[
                    :, half * HD : (half + 1) * HD
                ]
    for i in range(8):
        outgoing[i] = stage[i * 128 : (i + 1) * 128].astype(BF)

    phase1 = []
    for i in range(1, 8):
        p, there = xy_ctx(i)
        phase1.append(
            pltpu.make_async_remote_copy(
                src_ref=outgoing.at[p], dst_ref=plane.at[x, y],
                send_sem=p1_send.at[i - 1], recv_sem=p1_recv.at[i - 1],
                device_id={"ctx": there, "head": hd}, device_id_type=MESH,
            )
        )
    for copy in phase1:
        copy.start()
    plane[x, y] = outgoing[xy]

    mask_l = iota((HALF, 256), 1) <= iota((HALF, 256), 0)
    mask_h = iota((HALF, TOK), 1) <= iota((HALF, TOK), 0) + HALF

    def own_part(g, h, part):
        qs = pl.multiple_of(h * HD, HD)
        low = part == 0
        rs = slice(0, HALF) if low else slice(HALF, TOK)
        n = 256 if low else TOK
        st = {}

        def first():
            s = dot_t(q_ref[rs, pl.ds(qs, HD)], k_ref[:n, g * HD : (g + 1) * HD])
            st["s"] = jnp.where(mask_l if low else mask_h, s, -jnp.inf)
            st["m"] = jnp.max(st["s"], 1, keepdims=True)

        def second():
            w = jnp.exp2((st["s"] - st["m"]) * LOG2E_SCALE).astype(BF)
            (wl if low else wh)[h] = w
            m1[h, rs] = jnp.broadcast_to(st["m"], (HALF, HD))
            ot1[h, rs] = dot(w, with_ones(v_ref[:n, g * HD : (g + 1) * HD]))

        return [first, second]

    for g in range(G):
        loads[5 + g].wait()

        def own_heads(i, carry, g=g):
            units = []
            for u in range(4):
                h = g * QPK + i * 4 + u
                units += [own_part(g, h, 0), own_part(g, h, 1)]
            emit(units, 2)
            return carry

        lax.fori_loop(0, QPK // 4, own_heads, 0)

    for i in range(1, 8):
        p, _ = xy_ctx(-i)
        pltpu.make_async_remote_copy(
            src_ref=outgoing.at[p], dst_ref=plane.at[lax.div(p, 2), lax.rem(p, 2)],
            send_sem=p1_send.at[i - 1], recv_sem=p1_recv.at[i - 1],
            device_id={"ctx": xy_ctx(-i)[1], "head": hd}, device_id_type=MESH,
        ).wait_recv()
    phase2 = []
    for i in range(1, 8):
        p, there = z_ctx(i)
        phase2.append(
            pltpu.make_async_remote_copy(
                src_ref=plane.at[:, :, pl.ds(pl.multiple_of(p * 16, 16), 16), :],
                dst_ref=cache_hbm.at[:, z],
                send_sem=p2_send.at[i - 1], recv_sem=p2_recv.at[i - 1],
                device_id={"ctx": there, "head": hd}, device_id_type=MESH,
            )
        )
    for copy in phase2:
        copy.start()
    cache_own = pltpu.make_async_copy(
        plane.at[:, :, pl.ds(pl.multiple_of(z * 16, 16), 16), :], cache_hbm.at[:, z], out_sem.at[2]
    )
    cache_own.start()

    for w in range(2):
        near_a[w].wait_recv()
        near_b[w].wait_recv()

    out_copies = [
        pltpu.make_async_copy(
            out_ref.at[:, pl.ds(g * QPK * HD, QPK * HD)],
            out_hbm.at[:, pl.ds(g * QPK * HD, QPK * HD)],
            out_sem.at[g],
        )
        for g in range(G)
    ]

    def near_part(g, h, rs, n, acc):
        qs = pl.multiple_of(h * HD, HD)
        st = {}

        def first():
            if n:
                st["s"] = dot_t(q_ref[rs, pl.ds(qs, HD)], kn_ref[:n, g * HD : (g + 1) * HD])
                st["m"] = jnp.maximum(m1[h, rs], jnp.max(st["s"], 1, keepdims=True))

        def second():
            if n:
                w = jnp.exp2((st["s"] - st["m"][:, :1]) * LOG2E_SCALE).astype(BF)
                st["w"] = w
                st["ot"] = dot(w, with_ones(vn_ref[:n, g * HD : (g + 1) * HD]))

        def third():
            o1 = ot1[h, rs]
            if n:
                a = jnp.exp2((m1[h, rs] - st["m"]) * LOG2E_SCALE)
                inv = 1.0 / (a * o1[:, HD:] + st["ot"][:, HD:])
                o = (a * o1[:, :HD] + st["ot"][:, :HD]) * inv
                f = a * inv
                s = column_sum(st["w"], inv)
                for i in range(0, n, TOK):
                    part = s[:, i : min(i + TOK, n)]
                    if part.shape[1] < TOK:
                        part = jnp.concatenate(
                            [part, jnp.zeros((8, TOK - part.shape[1]), F32)], 1
                        )
                    acc[1 + i // TOK] = acc[1 + i // TOK] + part
            else:
                f = 1.0 / o1[:, HD:]
                o = o1[:, :HD] * f
            out_ref[rs, pl.ds(qs, HD)] = o.astype(BF)
            if rs.start < HALF:
                s = column_sum(wl[h], f[:HALF])
                acc[0] = acc[0] + jnp.concatenate([s, jnp.zeros((8, TOK - 256), F32)], 1)
            if rs.stop > HALF:
                acc[0] = acc[0] + column_sum(wh[h], f[HALF - rs.start :])

        return [first, second, third]

    def near_attention(parts, unroll):
        zero = jnp.zeros((8, TOK), F32)
        carry = (zero, zero, zero)
        for g in range(G):

            def heads(i, carry, g=g):
                acc = list(carry)
                units = []
                for u in range(unroll):
                    for rs, n in parts:
                        units.append(near_part(g, g * QPK + i * unroll + u, rs, n, acc))
                emit(units, 0)
                return tuple(acc)

            carry = lax.fori_loop(0, QPK // unroll, heads, carry)
            out_copies[g].start()
        col_own[...] = carry[0]
        col_near[0] = carry[1]
        col_near[1] = carry[2]

    @pl.when(c >= 2)
    def _():
        near_attention([(slice(0, TOK), TOK)], 8)

    @pl.when(c == 1)
    def _():
        for copy in far_b:
            copy.wait_recv()
        near_attention([(slice(0, HALF), HALF), (slice(HALF, TOK), 3 * HALF)], 8)

    @pl.when(c == 0)
    def _():
        for copy in far_b + far_a:
            copy.wait_recv()
        near_attention([(slice(0, HALF), 0), (slice(HALF, TOK), 4 * HALF)], 8)

    first = jnp.sum(col_near[0], 0, keepdims=True)
    second = jnp.sum(col_near[1], 0, keepdims=True)
    low = iota((1, TOK), 1) < HALF
    col_send[0] = jnp.sum(col_own[...], 0, keepdims=True)
    col_send[1] = jnp.where(low, first, second)
    col_send[2] = pltpu.roll(jnp.where(low, second, first), HALF, 1)
    sends = []
    for delta in range(3):
        for i in range(4):
            if delta or i:
                sends.append(
                    pltpu.make_async_remote_copy(
                        src_ref=col_send.at[delta], dst_ref=col_recv.at[delta * 4 + i],
                        send_sem=ks_send.at[delta * 4 + i], recv_sem=ks_recv.at[delta * 4 + i],
                        device_id={"ctx": ctx(-delta), "head": head_of(i)}, device_id_type=MESH,
                    )
                )
    for copy in sends:
        copy.start()
    for copy in sends:
        copy.wait_recv()
    total = col_send[0]
    for i in range(1, 12):
        total = total + col_recv[i]
    score_ref[...] = total * (1.0 / QH)
    score_copy = pltpu.make_async_copy(score_ref, score_hbm, out_sem.at[3])
    score_copy.start()

    for copy in phase2:
        copy.wait_send()
    for i in range(1, 8):
        p, there = z_ctx(-i)
        pltpu.make_async_remote_copy(
            src_ref=plane.at[:, :, pl.ds(pl.multiple_of(p * 16, 16), 16), :],
            dst_ref=cache_hbm.at[:, p],
            send_sem=p2_send.at[i - 1], recv_sem=p2_recv.at[i - 1],
            device_id={"ctx": there, "head": hd}, device_id_type=MESH,
        ).wait_recv()
    for copy in near_a + near_b + phase1 + sends:
        copy.wait_send()

    @pl.when(c >= N_CTX - 2)
    def _():
        for copy in far_b:
            copy.wait_send()

    @pl.when(c == N_CTX - 1)
    def _():
        for copy in far_a:
            copy.wait_send()

    for copy in out_copies + [cache_own, score_copy]:
        copy.wait()


def on_device(queries, keys, values, keep_rows, keep_dest, keep_count):
    anyspace = pl.BlockSpec(memory_space=pl.ANY)
    dma = pltpu.SemaphoreType.DMA
    attended, scores, cache = pl.pallas_call(
        kernel,
        name="window",
        out_shape=[
            jax.ShapeDtypeStruct((TOK, HEADS * HD), BF),
            jax.ShapeDtypeStruct((1, TOK), F32),
            jax.ShapeDtypeStruct((4, 8, 2, 16, HD), BF),
        ],
        in_specs=[anyspace] * 6,
        out_specs=[anyspace] * 3,
        scratch_shapes=[
            pltpu.VMEM((TOK, HEADS * HD), BF),
            pltpu.VMEM((TOK, G * HD), BF),
            pltpu.VMEM((TOK, G * HD), BF),
            pltpu.VMEM((1, G, N_CTX, KB), jnp.int32),
            pltpu.VMEM((1, G, N_CTX), jnp.int32),
            pltpu.VMEM((1, G, N_CTX), jnp.int32),
            pltpu.VMEM((4 * HALF, G * HD), BF),
            pltpu.VMEM((4 * HALF, G * HD), BF),
            pltpu.VMEM((N_CTX * 16, HD), F32),
            pltpu.VMEM((8, 128, HD), BF),
            pltpu.VMEM((4, 2, 128, HD), BF),
            pltpu.VMEM((TOK, HEADS * HD), BF),
            pltpu.VMEM((HEADS, TOK, 2 * HD), F32),
            pltpu.VMEM((HEADS, TOK, HD), F32),
            pltpu.VMEM((HEADS, HALF, 256), BF),
            pltpu.VMEM((HEADS, HALF, TOK), BF),
            pltpu.VMEM((8, TOK), F32),
            pltpu.VMEM((2, 8, TOK), F32),
            pltpu.VMEM((3, 1, TOK), F32),
            pltpu.VMEM((12, 1, TOK), F32),
            pltpu.VMEM((1, TOK), F32),
            dma((7,)), dma((4,)),
            dma((2, 4)), dma((2, 4)),
            dma((7,)), dma((7,)), dma((7,)), dma((7,)),
            dma((12,)), dma((12,)),
        ],
        compiler_params=pltpu.CompilerParams(
            collective_id=0, has_side_effects=True, vmem_limit_bytes=40 << 20
        ),
        cost_estimate=pl.CostEstimate(
            flops=2_200_000_000, bytes_accessed=4_000_000, transcendentals=4_200_000
        ),
    )(queries, keys, values, keep_rows, keep_dest, keep_count)
    cache = cache.reshape(N_CTX, KB, 2, G, HD).transpose(0, 1, 3, 2, 4)
    return attended, scores.reshape(TOK), cache.reshape(1, N_CTX, KB, G, 2 * HD)


def solution(mesh):
    return jax.shard_map(
        on_device,
        mesh=mesh,
        in_specs=(
            P("ctx", "head"),
            P("ctx", "head"),
            P("ctx", "head"),
            P("ctx", "head", None, None),
            P("ctx", "head", None),
            P("ctx", "head", None),
        ),
        out_specs=(P("ctx", "head"), P("ctx"), P("ctx", None, None, "head", None)),
        check_vma=False,
    )
```

```python
import jax
import jax.numpy as jnp
from jax import lax
from jax.experimental import pallas as pl
from jax.experimental.pallas import tpu as pltpu
from jax.sharding import PartitionSpec as P

HD = 128
KB = 4
QH = 64
TOK = 384
HALF = 192
G = 2
QPK = 8
HEADS = G * QPK
N_CTX = 64
F32 = jnp.float32
BF = jnp.bfloat16
LOG2E_SCALE = HD**-0.5 * 1.4426950408889634
MESH = pl.DeviceIdType.MESH


def dot(a, b):
    return lax.dot_general(a, b, (((1,), (0,)), ((), ())), preferred_element_type=F32)


def dot_t(a, b):
    return lax.dot_general(a, b, (((1,), (1,)), ((), ())), preferred_element_type=F32)


def iota(shape, dim):
    return lax.broadcasted_iota(jnp.int32, shape, dim)


def with_ones(v):
    return jnp.concatenate([v, jnp.ones(v.shape, BF)], 1)


def column_sum(w, f):
    r, n = w.shape
    return jnp.sum((w.astype(F32) * f[:, :1]).reshape(r // 8, 8, n), 0)


def emit(units, skew):
    stages = max(len(u) for u in units)
    for t in range(len(units) + (stages - 1) * skew):
        for k in range(stages):
            i = t - k * skew
            if 0 <= i < len(units) and k < len(units[i]):
                units[i][k]()


def kernel(
    q_hbm, k_hbm, v_hbm, rows_hbm, dest_hbm, count_hbm,
    out_ref, score_ref, cache_ref,
    q_ref, k_ref, v_ref, rows_ref, dest_ref, count_ref,
    kn_ref, vn_ref, stage, outgoing,
    ot1, m1, wl, wh, col_own, col_near, col_send, col_recv,
    in_sem, cache_send, cache_recv, kv_send, kv_recv, relay_send,
    ks_send, ks_recv,
):
    c = lax.axis_index("ctx")
    hd = lax.axis_index("head")
    x = lax.div(c, 16)
    z = lax.rem(lax.div(c, 2), 8)
    y = lax.rem(c, 2)
    odd = y == 1
    even = y == 0

    def ctx(delta):
        return lax.rem(c + delta + N_CTX, N_CTX)

    def head_of(i):
        return lax.rem(hd + i, 4)

    barrier = pltpu.get_barrier_semaphore()
    def greet(a, b):
        pl.semaphore_signal(barrier, inc=1, device_id={"ctx": a, "head": b}, device_id_type=MESH)

    def greet_row(i, carry):
        greet(ctx(i), hd)
        return carry

    lax.fori_loop(1, N_CTX, greet_row, 0)
    greeted = N_CTX - 1
    for delta in range(3):
        for i in range(1, 4):
            greet(ctx(delta), head_of(i))
            greeted += 1

    @pl.when(c == 1)
    def _():
        vn_ref[3 * HALF :, :] = jnp.zeros((HALF, G * HD), BF)

    loads = [
        pltpu.make_async_copy(src, dst, in_sem.at[i])
        for i, (src, dst) in enumerate(
            [
                (k_hbm, k_ref), (v_hbm, v_ref), (rows_hbm, rows_ref), (dest_hbm, dest_ref),
                (count_hbm, count_ref),
                (q_hbm.at[:, pl.ds(0, QPK * HD)], q_ref.at[:, pl.ds(0, QPK * HD)]),
                (q_hbm.at[:, pl.ds(QPK * HD, QPK * HD)], q_ref.at[:, pl.ds(QPK * HD, QPK * HD)]),
            ]
        )
    ]
    for load in loads:
        load.start()

    def kv_copy(w, g, slot, row, delta):
        cols = pl.ds(g * HD, HD)
        return pltpu.make_async_remote_copy(
            src_ref=(k_hbm, v_hbm)[w].at[pl.ds(row, HALF), cols],
            dst_ref=(kn_ref, vn_ref)[w].at[pl.ds(slot * HALF, HALF), cols],
            send_sem=kv_send.at[w, g, slot], recv_sem=kv_recv.at[w, g, slot],
            device_id={"ctx": ctx(delta), "head": hd}, device_id_type=MESH,
        )

    def relay_copy(w, g, slot, to):
        cols = pl.ds(g * HD, HD)
        near = (kn_ref, vn_ref)[w]
        return pltpu.make_async_remote_copy(
            src_ref=near.at[pl.ds(slot * HALF, HALF), cols],
            dst_ref=near.at[pl.ds(to * HALF, HALF), cols],
            send_sem=relay_send.at[w, g, slot], recv_sem=kv_recv.at[w, g, to],
            device_id={"ctx": ctx(-1), "head": hd}, device_id_type=MESH,
        )

    send_a = [[kv_copy(w, g, 0, 0, 1) for w in range(2)] for g in range(G)]
    send_b = [[kv_copy(w, g, 1, 0, 2) for w in range(2)] for g in range(G)]
    send_far = [[kv_copy(w, g, 2, HALF, 2) for w in range(2)] for g in range(G)]
    relay_low = [[relay_copy(w, g, 1, 0) for w in range(2)] for g in range(G)]
    relay_high = [[relay_copy(w, g, 2, 3) for w in range(2)] for g in range(G)]

    def send_blocks():
        for g in range(G):
            for copy in send_b[g]:
                copy.start()

            @pl.when(even)
            def _():
                for copy in send_a[g]:
                    copy.start()

            @pl.when(c >= N_CTX - 2)
            def _():
                for copy in send_far[g]:
                    copy.start()

    def relay(g):
        @pl.when(odd)
        def _():
            for w in range(2):
                send_b[g][w].wait_recv()
                relay_low[g][w].start()

        @pl.when(c == 1)
        def _():
            for w in range(2):
                send_far[g][w].wait_recv()
                relay_high[g][w].start()

    def wait_blocks(g):
        @pl.when(even)
        def _():
            for copy in send_b[g]:
                copy.wait_recv()

        for copy in send_a[g]:
            copy.wait_recv()

        @pl.when(c == 0)
        def _():
            for w in range(2):
                send_far[g][w].wait_recv()
                relay_high[g][w].wait_recv()

    def compact():
        for load in loads[:5]:
            load.wait()
        order = iota((N_CTX, N_CTX), 0)
        lane = iota((N_CTX, TOK), 1).astype(F32)
        for g in range(G):
            match = dest_ref[0, g : g + 1, :] == order
            live = jnp.sum(
                jnp.where(match, count_ref[0, g : g + 1, :].astype(F32), 0.0), 1, keepdims=True
            )
            match = jnp.where(match, 1.0, 0.0).astype(BF)
            rows = rows_ref[0, g]
            high = dot_t(match, (rows >> 4).astype(F32).astype(BF))
            low = dot_t(match, (rows & 15).astype(F32).astype(BF))
            rows = high * 16.0 + low
            pair = jnp.concatenate(
                [k_ref[:, g * HD : (g + 1) * HD], v_ref[:, g * HD : (g + 1) * HD]], 1
            )
            for t in range(KB):
                row = jnp.where(live > t, rows[:, t : t + 1], -1.0)
                pick = jnp.where(row == lane, 1.0, 0.0).astype(BF)
                picked = dot(pick, pair)
                for half in range(2):
                    stage[pl.ds(t * 4 + half * 2 + g, N_CTX, stride=16), :] = picked[
                        :, half * HD : (half + 1) * HD
                    ]
        outgoing[...] = stage[...].reshape(N_CTX, 16, HD).astype(BF)

    def send_block(to):
        @pl.when(to != c)
        def _():
            pltpu.make_async_remote_copy(
                src_ref=outgoing.at[to], dst_ref=cache_ref.at[c],
                send_sem=cache_send, recv_sem=cache_recv,
                device_id={"ctx": to, "head": hd}, device_id_type=MESH,
            ).start()

    def send_layer(there):
        def body(i, carry):
            p = lax.rem(x * 2 + y + i, 8)
            send_block(lax.div(p, 2) * 16 + there * 2 + lax.rem(p, 2))
            return carry

        lax.fori_loop(0, 8, body, 0)

    def send_cache():
        send_layer(0)
        for i in range(8):
            there = lax.rem(z + i, 8)

            @pl.when(there != 0)
            def _():
                send_layer(there)

        cache_ref[c] = outgoing[c]

    mask_l = iota((HALF, 256), 1) <= iota((HALF, 256), 0)
    mask_h = iota((HALF, TOK), 1) <= iota((HALF, TOK), 0) + HALF

    def own_part(g, h, part):
        qs = pl.multiple_of(h * HD, HD)
        low = part == 0
        rs = slice(0, HALF) if low else slice(HALF, TOK)
        n = 256 if low else TOK
        st = {}

        def first():
            s = dot_t(q_ref[rs, pl.ds(qs, HD)], k_ref[:n, g * HD : (g + 1) * HD])
            st["s"] = jnp.where(mask_l if low else mask_h, s, -jnp.inf)
            st["m"] = jnp.max(st["s"], 1, keepdims=True)

        def second():
            w = jnp.exp2((st["s"] - st["m"]) * LOG2E_SCALE).astype(BF)
            (wl if low else wh)[h] = w
            m1[h, rs] = jnp.broadcast_to(st["m"], (HALF, HD))
            ot1[h, rs] = dot(w, with_ones(v_ref[:n, g * HD : (g + 1) * HD]))

        return [first, second]

    def own_attention(g):
        loads[5 + g].wait()

        def own_heads(i, carry):
            units = []
            for u in range(4):
                h = g * QPK + i * 4 + u
                units += [own_part(g, h, 0), own_part(g, h, 1)]
            emit(units, 2)
            return carry

        lax.fori_loop(0, QPK // 4, own_heads, 0)

    compact()
    pl.semaphore_wait(barrier, greeted)
    send_blocks()
    send_cache()
    own_attention(0)
    relay(0)
    own_attention(1)

    @pl.when(c != 1)
    def _():
        relay(1)

    def near_part(g, h, rs, live, acc):
        n = (live + 127) // 128 * 128
        qs = pl.multiple_of(h * HD, HD)
        st = {}

        def first():
            if n:
                s = dot_t(q_ref[rs, pl.ds(qs, HD)], kn_ref[:n, g * HD : (g + 1) * HD])
                if live < n:
                    s = jnp.where(iota(s.shape, 1) < live, s, -jnp.inf)
                st["s"] = s
                st["m"] = jnp.maximum(m1[h, rs], jnp.max(st["s"], 1, keepdims=True))

        def second():
            if n:
                w = jnp.exp2((st["s"] - st["m"][:, :1]) * LOG2E_SCALE).astype(BF)
                st["w"] = w
                st["ot"] = dot(w, with_ones(vn_ref[:n, g * HD : (g + 1) * HD]))

        def third():
            o1 = ot1[h, rs]
            if n:
                a = jnp.exp2((m1[h, rs] - st["m"]) * LOG2E_SCALE)
                inv = 1.0 / (a * o1[:, HD:] + st["ot"][:, HD:])
                o = (a * o1[:, :HD] + st["ot"][:, :HD]) * inv
                f = a * inv
                s = column_sum(st["w"], inv)
                for i in range(0, n, TOK):
                    part = s[:, i : min(i + TOK, n)]
                    if part.shape[1] < TOK:
                        part = jnp.concatenate(
                            [part, jnp.zeros((8, TOK - part.shape[1]), F32)], 1
                        )
                    acc[1 + i // TOK] = acc[1 + i // TOK] + part
            else:
                f = 1.0 / o1[:, HD:]
                o = o1[:, :HD] * f
            out_ref[rs, pl.ds(qs, HD)] = o.astype(BF)
            if rs.start < HALF:
                s = column_sum(wl[h], f[:HALF])
                acc[0] = acc[0] + jnp.concatenate([s, jnp.zeros((8, TOK - 256), F32)], 1)
            if rs.stop > HALF:
                acc[0] = acc[0] + column_sum(wh[h], f[HALF - rs.start :])

        return [first, second, third]

    def near_attention(parts, unroll, shard_one=False):
        zero = jnp.zeros((8, TOK), F32)
        carry = (zero, zero, zero)
        for g in range(G):
            if g and shard_one:
                relay(g)
            wait_blocks(g)

            def heads(i, carry, g=g):
                acc = list(carry)
                units = []
                for u in range(unroll):
                    for rs, n in parts:
                        units.append(near_part(g, g * QPK + i * unroll + u, rs, n, acc))
                emit(units, 0)
                return tuple(acc)

            carry = lax.fori_loop(0, QPK // unroll, heads, carry)
        col_own[...] = carry[0]
        col_near[0] = carry[1]
        col_near[1] = carry[2]

    @pl.when(c >= 2)
    def _():
        near_attention([(slice(0, TOK), TOK)], 8)

    @pl.when(c == 1)
    def _():
        near_attention([(slice(0, HALF), HALF), (slice(HALF, TOK), 3 * HALF)], 8, True)

    @pl.when(c == 0)
    def _():
        near_attention([(slice(0, HALF), 0), (slice(HALF, TOK), 4 * HALF)], 8)

    first = jnp.sum(col_near[0], 0, keepdims=True)
    second = jnp.sum(col_near[1], 0, keepdims=True)
    low = iota((1, TOK), 1) < HALF
    col_send[0] = jnp.sum(col_own[...], 0, keepdims=True)
    col_send[1] = jnp.where(low, first, second)
    col_send[2] = pltpu.roll(jnp.where(low, second, first), HALF, 1)
    sends = []
    for delta in range(3):
        for i in range(4):
            if delta or i:
                sends.append(
                    pltpu.make_async_remote_copy(
                        src_ref=col_send.at[delta], dst_ref=col_recv.at[delta * 4 + i],
                        send_sem=ks_send.at[delta * 4 + i], recv_sem=ks_recv.at[delta * 4 + i],
                        device_id={"ctx": ctx(-delta), "head": head_of(i)}, device_id_type=MESH,
                    )
                )
    for copy in sends:
        copy.start()
    for copy in sends:
        copy.wait_recv()
    total = col_send[0]
    for i in range(1, 12):
        total = total + col_recv[i]
    score_ref[...] = total * (1.0 / QH)

    others = cache_ref.at[pl.ds(0, N_CTX - 1)]
    pltpu.make_async_copy(others, others, cache_recv).wait()
    pltpu.make_async_copy(others, others, cache_send).wait()
    for copy in sends:
        copy.wait_send()
    for g in range(G):
        for copy in send_b[g]:
            copy.wait_send()

        @pl.when(even)
        def _():
            for copy in send_a[g]:
                copy.wait_send()

        @pl.when(odd)
        def _():
            for copy in relay_low[g]:
                copy.wait_send()

        @pl.when(c >= N_CTX - 2)
        def _():
            for copy in send_far[g]:
                copy.wait_send()

        @pl.when(c == 1)
        def _():
            for copy in relay_high[g]:
                copy.wait_send()


def tail(a_in, s_in, c_in, a_out, s_out, c_out, sem):
    copies = [
        pltpu.make_async_copy(a_in, a_out, sem.at[0]),
        pltpu.make_async_copy(c_in, c_out, sem.at[1]),
        pltpu.make_async_copy(s_in.at[0], s_out, sem.at[2]),
    ]
    for copy in copies:
        copy.start()
    for copy in copies:
        copy.wait()


def on_device(queries, keys, values, keep_rows, keep_dest, keep_count):
    dma = pltpu.SemaphoreType.DMA
    anywhere = pl.BlockSpec(memory_space=pl.ANY)
    operands = [queries, keys, values, keep_rows.transpose(0, 1, 3, 2), keep_dest, keep_count]
    results = pl.pallas_call(
        lambda *refs: kernel(*refs),
        name="window",
        out_shape=[
            jax.ShapeDtypeStruct((TOK, HEADS * HD), BF),
            jax.ShapeDtypeStruct((1, TOK), F32),
            jax.ShapeDtypeStruct((N_CTX, 16, HD), BF),
        ],
        in_specs=[anywhere] * 6,
        out_specs=[pl.BlockSpec(memory_space=pltpu.VMEM)] * 3,
        scratch_shapes=[
            pltpu.VMEM((TOK, HEADS * HD), BF),
            pltpu.VMEM((TOK, G * HD), BF),
            pltpu.VMEM((TOK, G * HD), BF),
            pltpu.VMEM((1, G, KB, N_CTX), jnp.int32),
            pltpu.VMEM((1, G, N_CTX), jnp.int32),
            pltpu.VMEM((1, G, N_CTX), jnp.int32),
            pltpu.VMEM((4 * HALF, G * HD), BF),
            pltpu.VMEM((4 * HALF, G * HD), BF),
            pltpu.VMEM((N_CTX * 16, HD), F32),
            pltpu.VMEM((N_CTX, 16, HD), BF),
            pltpu.VMEM((HEADS, TOK, 2 * HD), F32),
            pltpu.VMEM((HEADS, TOK, HD), F32),
            pltpu.VMEM((HEADS, HALF, 256), BF),
            pltpu.VMEM((HEADS, HALF, TOK), BF),
            pltpu.VMEM((8, TOK), F32),
            pltpu.VMEM((2, 8, TOK), F32),
            pltpu.VMEM((3, 1, TOK), F32),
            pltpu.VMEM((12, 1, TOK), F32),
            dma((7,)), dma, dma,
            dma((2, G, 4)), dma((2, G, 4)), dma((2, G, 4)),
            dma((12,)), dma((12,)),
        ],
        compiler_params=pltpu.CompilerParams(
            collective_id=0, has_side_effects=True, vmem_limit_bytes=40 << 20
        ),
        cost_estimate=pl.CostEstimate(
            flops=2_200_000_000, bytes_accessed=4_000_000, transcendentals=4_200_000
        ),
    )(*[pltpu.with_memory_space_constraint(v, pltpu.HBM) for v in operands])
    attended, scores, cache = pl.pallas_call(
        tail,
        name="tail",
        out_shape=[
            jax.ShapeDtypeStruct((TOK, HEADS * HD), BF),
            jax.ShapeDtypeStruct((TOK,), F32),
            jax.ShapeDtypeStruct((N_CTX, 16, HD), BF),
        ],
        in_specs=[anywhere] * 3,
        out_specs=[anywhere] * 3,
        scratch_shapes=[dma((3,))],
        compiler_params=pltpu.CompilerParams(vmem_limit_bytes=1 << 20),
    )(*results)
    cache = cache.reshape(N_CTX, KB, 2, G, HD).transpose(0, 1, 3, 2, 4)
    return attended, scores, cache.reshape(1, N_CTX, KB, G, 2 * HD)


def solution(mesh):
    return jax.shard_map(
        on_device,
        mesh=mesh,
        in_specs=(
            P("ctx", "head"),
            P("ctx", "head"),
            P("ctx", "head"),
            P("ctx", "head", None, None),
            P("ctx", "head", None),
            P("ctx", "head", None),
        ),
        out_specs=(P("ctx", "head"), P("ctx"), P("ctx", None, None, "head", None)),
        check_vma=False,
    )
```

```python
import jax
import jax.numpy as jnp
from jax import lax
from jax.experimental import pallas as pl
from jax.experimental.pallas import tpu as pltpu
from jax.sharding import PartitionSpec as P

HD = 128
KB = 4
QH = 64
TOK = 384
HALF = 192
G = 2
QPK = 8
HEADS = G * QPK
N_CTX = 64
F32 = jnp.float32
BF = jnp.bfloat16
LOG2E_SCALE = HD**-0.5 * 1.4426950408889634
MESH = pl.DeviceIdType.MESH
UNROLL = 8


def dot(a, b):
    return lax.dot_general(a, b, (((1,), (0,)), ((), ())), preferred_element_type=F32)


def dot_t(a, b):
    return lax.dot_general(a, b, (((1,), (1,)), ((), ())), preferred_element_type=F32)


def iota(shape, dim):
    return lax.broadcasted_iota(jnp.int32, shape, dim)


def with_ones(v):
    return jnp.concatenate([v, jnp.ones(v.shape, BF)], 1)


def column_sum(w, f):
    r, n = w.shape
    return jnp.sum((w.astype(F32) * f[:, :1]).reshape(r // 8, 8, n), 0)


def emit(units, skew):
    stages = max(len(u) for u in units)
    for t in range(len(units) + (stages - 1) * skew):
        for k in range(stages):
            i = t - k * skew
            if 0 <= i < len(units) and k < len(units[i]):
                units[i][k]()


def kernel(
    q_hbm, k_hbm, v_hbm, rows_hbm, dest_hbm, count_hbm,
    out_ref, score_ref, cache_ref,
    q_ref, k_ref, v_ref, rows_ref, dest_ref, count_ref,
    kn_ref, vn_ref, detour_ref, stage, outgoing,
    ot1, m1, m2, wl, wh, wm, col_send, col_recv,
    in_sem, cache_send, cache_recv, kv_send, kv_recv, relay_send, detour_send, detour_recv,
    ks_send, ks_recv,
):
    c = lax.axis_index("ctx")
    hd = lax.axis_index("head")
    x = lax.div(c, 16)
    z = lax.rem(lax.div(c, 2), 8)
    y = lax.rem(c, 2)
    odd = y == 1
    even = y == 0

    def ctx(delta):
        return lax.rem(c + delta + N_CTX, N_CTX)

    def head_of(i):
        return lax.rem(hd + i, 4)

    barrier = pltpu.get_barrier_semaphore()
    def greet(a, b):
        pl.semaphore_signal(barrier, inc=1, device_id={"ctx": a, "head": b}, device_id_type=MESH)

    def greet_row(i, carry):
        greet(ctx(i), hd)
        return carry

    lax.fori_loop(1, N_CTX, greet_row, 0)
    greeted = N_CTX - 1
    for delta in range(3):
        for i in range(1, 4):
            greet(ctx(delta), head_of(i))
            greeted += 1

    @pl.when(c == 1)
    def _():
        kn_ref[2 * HALF - 256 : HALF, :] = jnp.zeros((256 - HALF, G * HD), BF)
        vn_ref[2 * HALF - 256 : HALF, :] = jnp.zeros((256 - HALF, G * HD), BF)

    loads = [
        pltpu.make_async_copy(src, dst, in_sem.at[i])
        for i, (src, dst) in enumerate(
            [
                (k_hbm, k_ref), (v_hbm, v_ref), (rows_hbm, rows_ref), (dest_hbm, dest_ref),
                (count_hbm, count_ref),
                (q_hbm.at[:, pl.ds(0, QPK * HD)], q_ref.at[:, pl.ds(0, QPK * HD)]),
                (q_hbm.at[:, pl.ds(QPK * HD, QPK * HD)], q_ref.at[:, pl.ds(QPK * HD, QPK * HD)]),
            ]
        )
    ]
    for load in loads:
        load.start()

    def kv_copy(w, g, slot, row, delta):
        cols = pl.ds(g * HD, HD)
        return pltpu.make_async_remote_copy(
            src_ref=(k_hbm, v_hbm)[w].at[pl.ds(row, HALF), cols],
            dst_ref=(kn_ref, vn_ref)[w].at[pl.ds(slot * HALF, HALF), cols],
            send_sem=kv_send.at[w, g, slot], recv_sem=kv_recv.at[w, g, slot],
            device_id={"ctx": ctx(delta), "head": hd}, device_id_type=MESH,
        )

    def detour_copy(w, first):
        cols = pl.ds((G - 1) * HD, HD)
        rows = pl.ds(HALF, HALF) if first else pl.ds(0, HALF)
        return pltpu.make_async_remote_copy(
            src_ref=(k_hbm, v_hbm)[w].at[rows, cols] if first else detour_ref.at[w],
            dst_ref=detour_ref.at[w] if first else (kn_ref, vn_ref)[w].at[rows, cols],
            send_sem=detour_send.at[w],
            recv_sem=detour_recv.at[w] if first else kv_recv.at[w, G - 1, 0],
            device_id={"ctx": ctx(-1 if first else 2), "head": hd}, device_id_type=MESH,
        )

    def relay_copy(w, g, slot, to):
        cols = pl.ds(g * HD, HD)
        near = (kn_ref, vn_ref)[w]
        return pltpu.make_async_remote_copy(
            src_ref=near.at[pl.ds(slot * HALF, HALF), cols],
            dst_ref=near.at[pl.ds(to * HALF, HALF), cols],
            send_sem=relay_send.at[w, g, slot], recv_sem=kv_recv.at[w, g, to],
            device_id={"ctx": ctx(-1), "head": hd}, device_id_type=MESH,
        )

    send_a = [[kv_copy(w, g, 1, 0, 1) for w in range(2)] for g in range(G)]
    send_b = [[kv_copy(w, g, 2, 0, 2) for w in range(2)] for g in range(G)]
    send_far = [[kv_copy(w, g, 3, HALF, 2) for w in range(2)] for g in range(G)]
    relay_low = [[relay_copy(w, g, 2, 1) for w in range(2)] for g in range(G)]
    relay_high = [[relay_copy(w, g, 3, 0) for w in range(2)] for g in range(G)]
    detour = [[detour_copy(w, first) for w in range(2)] for first in (True, False)]

    def send_blocks():

        @pl.when(c == N_CTX - 1)
        def _():
            for copy in detour[0]:
                copy.start()

        for g in range(G):
            for copy in send_b[g]:
                copy.start()

            @pl.when(even)
            def _():
                for copy in send_a[g]:
                    copy.start()

            @pl.when(c >= N_CTX - 2)
            def _():
                for copy in send_far[g]:
                    copy.start()

    def pass_on(received, relayed):
        for w in range(2):
            received[w].wait_recv()
            relayed[w].start()

    def wait_all(*groups):
        for group in groups:
            for copy in group:
                copy.wait_recv()

    def relay(g):
        @pl.when((y == 1) & (c != 1))
        def _():
            pass_on(send_b[g], relay_low[g])

    def compact():
        for load in loads[:5]:
            load.wait()
        order = iota((N_CTX, N_CTX), 0)
        lane = iota((N_CTX, TOK), 1).astype(F32)
        for g in range(G):
            match = dest_ref[0, g : g + 1, :] == order
            live = jnp.sum(
                jnp.where(match, count_ref[0, g : g + 1, :].astype(F32), 0.0), 1, keepdims=True
            )
            match = jnp.where(match, 1.0, 0.0).astype(BF)
            rows = rows_ref[0, g]
            high = dot_t(match, (rows >> 4).astype(F32).astype(BF))
            low = dot_t(match, (rows & 15).astype(F32).astype(BF))
            rows = high * 16.0 + low
            pair = jnp.concatenate(
                [k_ref[:, g * HD : (g + 1) * HD], v_ref[:, g * HD : (g + 1) * HD]], 1
            )
            for t in range(KB):
                row = jnp.where(live > t, rows[:, t : t + 1], -1.0)
                pick = jnp.where(row == lane, 1.0, 0.0).astype(BF)
                picked = dot(pick, pair)
                for half in range(2):
                    stage[pl.ds(t * 4 + half * 2 + g, N_CTX, stride=16), :] = picked[
                        :, half * HD : (half + 1) * HD
                    ]
        outgoing[...] = stage[...].reshape(N_CTX, 16, HD).astype(BF)

    def send_block(to):
        @pl.when(to != c)
        def _():
            pltpu.make_async_remote_copy(
                src_ref=outgoing.at[to], dst_ref=cache_ref.at[c],
                send_sem=cache_send, recv_sem=cache_recv,
                device_id={"ctx": to, "head": hd}, device_id_type=MESH,
            ).start()

    def send_layer(there):
        def body(i, carry):
            p = lax.rem(x * 2 + y + i, 8)
            send_block(lax.div(p, 2) * 16 + there * 2 + lax.rem(p, 2))
            return carry

        lax.fori_loop(0, 8, body, 0)

    def send_cache():
        for i in range(8):
            send_layer(lax.rem(z + i, 8))

        cache_ref[c] = outgoing[c]

    mask_l = iota((HALF, 256), 1) <= iota((HALF, 256), 0)
    mask_h = iota((HALF, TOK), 1) <= iota((HALF, TOK), 0) + HALF

    def own_part(g, h, part):
        qs = pl.multiple_of(h * HD, HD)
        low = part == 0
        rs = slice(0, HALF) if low else slice(HALF, TOK)
        n = 256 if low else TOK
        st = {}

        def first():
            s = dot_t(q_ref[rs, pl.ds(qs, HD)], k_ref[:n, g * HD : (g + 1) * HD])
            st["s"] = jnp.where(mask_l if low else mask_h, s, -jnp.inf)
            st["m"] = jnp.max(st["s"], 1, keepdims=True)

        def second():
            w = jnp.exp2((st["s"] - st["m"]) * LOG2E_SCALE).astype(BF)
            (wl if low else wh)[h] = w
            m1[h, rs] = jnp.broadcast_to(st["m"], (HALF, HD))
            ot1[h, rs] = dot(w, with_ones(v_ref[:n, g * HD : (g + 1) * HD]))

        return [first, second]

    def own_attention(g):
        loads[5 + g].wait()

        def own_heads(i, carry):
            units = []
            for u in range(4):
                h = g * QPK + i * 4 + u
                units += [own_part(g, h, 0), own_part(g, h, 1)]
            emit(units, 2)
            return carry

        lax.fori_loop(0, QPK // 4, own_heads, 0)

    compact()

    @pl.when(z == 0)
    def _():
        for g in range(G):
            own_attention(g)

    pl.semaphore_wait(barrier, greeted)
    send_blocks()

    @pl.when(c != N_CTX - 2)
    def _():
        send_cache()

    @pl.when(z != 0)
    def _():
        own_attention(0)

    @pl.when(c == N_CTX - 2)
    def _():
        pass_on(*detour)
        send_cache()

    relay(0)

    @pl.when(z != 0)
    def _():
        own_attention(1)

    relay(1)

    def weights(g, h, rs, start, n, before, unused=0):
        keys = kn_ref[start : start + n, g * HD : (g + 1) * HD]
        s = dot_t(q_ref[rs, pl.ds(pl.multiple_of(h * HD, HD), HD)], keys)
        if unused:
            s = jnp.where(iota(s.shape, 1) >= unused, s, -jnp.inf)
        return s, jnp.maximum(before[h, rs], jnp.max(s, 1, keepdims=True))

    def products(g, s, m, start, n):
        w = jnp.exp2((s - m[:, :1]) * LOG2E_SCALE).astype(BF)
        return w, dot(w, with_ones(vn_ref[start : start + n, g * HD : (g + 1) * HD]))

    def add(acc, i, s):
        if s.shape[1] < TOK:
            s = jnp.concatenate([s, jnp.zeros((8, TOK - s.shape[1]), F32)], 1)
        acc[i] = acc[i] + s

    def middle_part(g, h, rs, start, n, acc, unused=0):
        st = {}

        def first():
            st["s"], st["m"] = weights(g, h, rs, start, n, m1, unused)

        def second():
            w, st["ot"] = products(g, st["s"], st["m"], start, n)
            wm[h, rs, :n] = w

        def third():
            a = jnp.exp2((m1[h, rs] - st["m"]) * LOG2E_SCALE)
            ot1[h, rs] = jnp.concatenate([a, a], 1) * ot1[h, rs] + st["ot"]
            m2[h, rs] = st["m"]

        return [first, second, third]

    def last_part(g, h, rs, start, n, acc, middle=0):
        st = {}
        before = m2 if middle else m1

        def first():
            if n:
                st["s"], st["m"] = weights(g, h, rs, start, n, before)

        def second():
            if n:
                st["w"], st["ot"] = products(g, st["s"], st["m"], start, n)

        def third():
            o1 = ot1[h, rs]
            if n:
                a = jnp.exp2((before[h, rs] - st["m"]) * LOG2E_SCALE)
                inv = 1.0 / (a * o1[:, HD:] + st["ot"][:, HD:])
                o = (a * o1[:, :HD] + st["ot"][:, :HD]) * inv
                f = a * inv
                s = column_sum(st["w"], inv)
                add(acc, 1, s[:, :TOK])
                if n > TOK:
                    add(acc, 2, s[:, TOK:])
            else:
                f = 1.0 / o1[:, HD:]
                o = o1[:, :HD] * f
            out_ref[rs, pl.ds(pl.multiple_of(h * HD, HD), HD)] = o.astype(BF)
            if middle:
                add(acc, 2, column_sum(wm[h, rs, :middle], f))
                f = jnp.exp2((m1[h, rs] - m2[h, rs]) * LOG2E_SCALE) * f
            if rs.start < HALF:
                add(acc, 0, column_sum(wl[h], f[:HALF]))
            if rs.stop > HALF:
                add(acc, 0, column_sum(wh[h], f[HALF - rs.start :]))

        return [first, second, third]

    def near_heads(g, parts, carry):
        def heads(i, carry):
            acc = list(carry)
            units = []
            for u in range(UNROLL):
                for part, args in parts:
                    units.append(part(g, g * QPK + i * UNROLL + u, *args[:3], acc, *args[3:]))
            emit(units, 0)
            return tuple(acc)

        return lax.fori_loop(0, QPK // UNROLL, heads, carry)

    def add_up(carry):
        return [jnp.sum(a, 0, keepdims=True) for a in carry]

    whole, low, high = slice(0, TOK), slice(0, HALF), slice(HALF, TOK)
    left = iota((1, TOK), 1) < HALF
    carry = (jnp.zeros((8, TOK), F32),) * 3

    @pl.when(c >= 2)
    def _():
        acc = carry
        for g in range(G):

            @pl.when(even)
            def _():
                wait_all(send_b[g])

            wait_all(send_a[g])
            acc = near_heads(g, [(last_part, (whole, HALF, TOK))], acc)
        own, near, _ = add_up(acc)
        col_send[0] = own
        col_send[1] = jnp.where(left, near, 0.0)
        col_send[2] = pltpu.roll(jnp.where(left, 0.0, near), HALF, 1)

    @pl.when(c == 1)
    def _():
        acc = carry
        middle = [(middle_part, (whole, 2 * HALF - 256, 256, 256 - HALF))]
        last = [(last_part, (low, 0, 0, 256)), (last_part, (high, 2 * HALF, TOK, 256))]
        pass_on(send_b[0], relay_low[0])
        wait_all(send_a[0])
        acc = near_heads(0, middle, acc)
        pass_on(send_far[0], relay_high[0])
        wait_all(send_a[1])
        acc = near_heads(1, middle, acc)
        pass_on(send_b[1], relay_low[1])
        acc = near_heads(0, last, acc)
        wait_all(send_far[1])
        acc = near_heads(1, last, acc)
        col_send[0], col_send[2], near = add_up(acc)
        col_send[1] = pltpu.roll(near, TOK - (256 - HALF), 1)

    @pl.when(c == 0)
    def _():
        acc = carry
        parts = [(last_part, (low, 0, 0)), (last_part, (high, 0, 2 * TOK))]
        for g in range(G):
            wait_all(send_b[g], send_far[g], send_a[g], relay_high[g])
            acc = near_heads(g, parts, acc)
        own, first, second = add_up(acc)
        first = pltpu.roll(first, HALF, 1)
        col_send[0] = own
        col_send[1] = first
        col_send[2] = second

    sends = []
    for delta in range(3):
        for i in range(4):
            if delta or i:
                sends.append(
                    pltpu.make_async_remote_copy(
                        src_ref=col_send.at[delta], dst_ref=col_recv.at[delta * 4 + i],
                        send_sem=ks_send.at[delta * 4 + i], recv_sem=ks_recv.at[delta * 4 + i],
                        device_id={"ctx": ctx(-delta), "head": head_of(i)}, device_id_type=MESH,
                    )
                )
    for copy in sends:
        copy.start()
    for copy in sends:
        copy.wait_recv()
    total = col_send[0]
    for i in range(1, 12):
        total = total + col_recv[i]
    score_ref[...] = total * (1.0 / QH)

    others = cache_ref.at[pl.ds(0, N_CTX - 1)]
    pltpu.make_async_copy(others, others, cache_recv).wait()
    pltpu.make_async_copy(others, others, cache_send).wait()
    for copy in sends:
        copy.wait_send()
    for g in range(G):
        for copy in send_b[g]:
            copy.wait_send()

        @pl.when(even)
        def _():
            for copy in send_a[g]:
                copy.wait_send()

        @pl.when(odd)
        def _():
            for copy in relay_low[g]:
                copy.wait_send()

        @pl.when(c >= N_CTX - 2)
        def _():
            for copy in send_far[g]:
                copy.wait_send()

    @pl.when(c == 1)
    def _():
        for copy in relay_high[0]:
            copy.wait_send()

    @pl.when(c == N_CTX - 1)
    def _():
        for copy in detour[0]:
            copy.wait_send()

    @pl.when(c == N_CTX - 2)
    def _():
        for copy in detour[1]:
            copy.wait_send()


def tail(a_in, s_in, c_in, a_out, s_out, c_out, sem):
    copies = [
        pltpu.make_async_copy(a_in, a_out, sem.at[0]),
        pltpu.make_async_copy(c_in, c_out, sem.at[1]),
        pltpu.make_async_copy(s_in.at[0], s_out, sem.at[2]),
    ]
    for copy in copies:
        copy.start()
    for copy in copies:
        copy.wait()


def on_device(queries, keys, values, keep_rows, keep_dest, keep_count):
    dma = pltpu.SemaphoreType.DMA
    anywhere = pl.BlockSpec(memory_space=pl.ANY)
    operands = [queries, keys, values, keep_rows.transpose(0, 1, 3, 2), keep_dest, keep_count]
    results = pl.pallas_call(
        lambda *refs: kernel(*refs),
        name="window",
        out_shape=[
            jax.ShapeDtypeStruct((TOK, HEADS * HD), BF),
            jax.ShapeDtypeStruct((1, TOK), F32),
            jax.ShapeDtypeStruct((N_CTX, 16, HD), BF),
        ],
        in_specs=[anywhere] * 6,
        out_specs=[pl.BlockSpec(memory_space=pltpu.VMEM)] * 3,
        scratch_shapes=[
            pltpu.VMEM((TOK, HEADS * HD), BF),
            pltpu.VMEM((TOK, G * HD), BF),
            pltpu.VMEM((TOK, G * HD), BF),
            pltpu.VMEM((1, G, KB, N_CTX), jnp.int32),
            pltpu.VMEM((1, G, N_CTX), jnp.int32),
            pltpu.VMEM((1, G, N_CTX), jnp.int32),
            pltpu.VMEM((4 * HALF, G * HD), BF),
            pltpu.VMEM((4 * HALF, G * HD), BF),
            pltpu.VMEM((2, HALF, HD), BF),
            pltpu.VMEM((N_CTX * 16, HD), F32),
            pltpu.VMEM((N_CTX, 16, HD), BF),
            pltpu.VMEM((HEADS, TOK, 2 * HD), F32),
            pltpu.VMEM((HEADS, TOK, HD), F32),
            pltpu.VMEM((HEADS, TOK, HD), F32),
            pltpu.VMEM((HEADS, HALF, 256), BF),
            pltpu.VMEM((HEADS, HALF, TOK), BF),
            pltpu.VMEM((HEADS, TOK, 256), BF),
            pltpu.VMEM((3, 1, TOK), F32),
            pltpu.VMEM((12, 1, TOK), F32),
            dma((7,)), dma, dma,
            dma((2, G, 4)), dma((2, G, 4)), dma((2, G, 4)), dma((2,)), dma((2,)),
            dma((12,)), dma((12,)),
        ],
        compiler_params=pltpu.CompilerParams(
            collective_id=0, has_side_effects=True, vmem_limit_bytes=40 << 20
        ),
        cost_estimate=pl.CostEstimate(
            flops=2_200_000_000, bytes_accessed=4_000_000, transcendentals=4_200_000
        ),
    )(*[pltpu.with_memory_space_constraint(v, pltpu.HBM) for v in operands])
    attended, scores, cache = pl.pallas_call(
        tail,
        name="tail",
        out_shape=[
            jax.ShapeDtypeStruct((TOK, HEADS * HD), BF),
            jax.ShapeDtypeStruct((TOK,), F32),
            jax.ShapeDtypeStruct((N_CTX, 16, HD), BF),
        ],
        in_specs=[anywhere] * 3,
        out_specs=[anywhere] * 3,
        scratch_shapes=[dma((3,))],
        compiler_params=pltpu.CompilerParams(vmem_limit_bytes=1 << 20),
    )(*results)
    cache = cache.reshape(N_CTX, KB, 2, G, HD).transpose(0, 1, 3, 2, 4)
    return attended, scores, cache.reshape(1, N_CTX, KB, G, 2 * HD)


def solution(mesh):
    return jax.shard_map(
        on_device,
        mesh=mesh,
        in_specs=(
            P("ctx", "head"),
            P("ctx", "head"),
            P("ctx", "head"),
            P("ctx", "head", None, None),
            P("ctx", "head", None),
            P("ctx", "head", None),
        ),
        out_specs=(P("ctx", "head"), P("ctx"), P("ctx", None, None, "head", None)),
        check_vma=False,
    )
```

```python
import jax
import jax.numpy as jnp
from jax import lax
from jax.experimental import pallas as pl
from jax.experimental.pallas import tpu as pltpu
from jax.sharding import PartitionSpec as P

HD = 128
KB = 4
QH = 64
TOK = 384
HALF = 192
G = 2
QPK = 8
HEADS = G * QPK
N_CTX = 64
F32 = jnp.float32
BF = jnp.bfloat16
LOG2E_SCALE = HD**-0.5 * 1.4426950408889634
MESH = pl.DeviceIdType.MESH
UNROLL = 8


def dot(a, b):
    return lax.dot_general(a, b, (((1,), (0,)), ((), ())), preferred_element_type=F32)


def dot_t(a, b):
    return lax.dot_general(a, b, (((1,), (1,)), ((), ())), preferred_element_type=F32)


def iota(shape, dim):
    return lax.broadcasted_iota(jnp.int32, shape, dim)


def with_ones(v):
    return jnp.concatenate([v, jnp.ones(v.shape, BF)], 1)


def column_sum(w, f):
    r, n = w.shape
    return jnp.sum((w.astype(F32) * f[:, :1]).reshape(r // 8, 8, n), 0)


def emit(units, skew):
    stages = max(len(u) for u in units)
    for t in range(len(units) + (stages - 1) * skew):
        for k in range(stages):
            i = t - k * skew
            if 0 <= i < len(units) and k < len(units[i]):
                units[i][k]()


def kernel(
    q_hbm, k_hbm, v_hbm, rows_hbm, dest_hbm, count_hbm,
    out_ref, score_ref, cache_ref,
    q_ref, k_ref, v_ref, rows_ref, dest_ref, count_ref,
    kn_ref, vn_ref, detour_ref, stage, outgoing,
    ot1, m1, m2, wl, wh, wm, col_send, col_recv,
    in_sem, cache_send, cache_recv, kv_send, kv_recv, relay_send, detour_send, detour_recv, forward_send,
    ks_send, ks_recv,
):
    c = lax.axis_index("ctx")
    hd = lax.axis_index("head")
    x = lax.div(c, 16)
    z = lax.rem(lax.div(c, 2), 8)
    y = lax.rem(c, 2)
    odd = y == 1
    even = y == 0

    def ctx(delta):
        return lax.rem(c + delta + N_CTX, N_CTX)

    def head_of(i):
        return lax.rem(hd + i, 4)

    barrier = pltpu.get_barrier_semaphore()
    def greet(a, b):
        pl.semaphore_signal(barrier, inc=1, device_id={"ctx": a, "head": b}, device_id_type=MESH)

    def greet_row(i, carry):
        greet(ctx(i), hd)
        return carry

    lax.fori_loop(1, N_CTX, greet_row, 0)
    greeted = N_CTX - 1
    for delta in range(3):
        for i in range(1, 4):
            greet(ctx(delta), head_of(i))
            greeted += 1

    @pl.when(c == 1)
    def _():
        kn_ref[2 * HALF - 256 : HALF, :] = jnp.zeros((256 - HALF, G * HD), BF)
        vn_ref[2 * HALF - 256 : HALF, :] = jnp.zeros((256 - HALF, G * HD), BF)

    loads = [
        pltpu.make_async_copy(src, dst, in_sem.at[i])
        for i, (src, dst) in enumerate(
            [
                (k_hbm, k_ref), (v_hbm, v_ref), (rows_hbm, rows_ref), (dest_hbm, dest_ref),
                (count_hbm, count_ref),
                (q_hbm.at[:, pl.ds(0, QPK * HD)], q_ref.at[:, pl.ds(0, QPK * HD)]),
                (q_hbm.at[:, pl.ds(QPK * HD, QPK * HD)], q_ref.at[:, pl.ds(QPK * HD, QPK * HD)]),
            ]
        )
    ]
    for load in loads:
        load.start()

    def kv_copy(w, g, slot, row, delta):
        cols = pl.ds(g * HD, HD)
        return pltpu.make_async_remote_copy(
            src_ref=(k_hbm, v_hbm)[w].at[pl.ds(row, HALF), cols],
            dst_ref=(kn_ref, vn_ref)[w].at[pl.ds(slot * HALF, HALF), cols],
            send_sem=kv_send.at[w, g, slot], recv_sem=kv_recv.at[w, g, slot],
            device_id={"ctx": ctx(delta), "head": hd}, device_id_type=MESH,
        )

    detours = [(0, 0), (1, 0), (1, 3), (0, 3), (1, 3)]
    cols_last = pl.ds((G - 1) * HD, HD)

    def detour_copy(i):
        w, slot = detours[i]
        step = i % 3
        return pltpu.make_async_remote_copy(
            src_ref=(k_hbm, v_hbm)[w].at[pl.ds(HALF, HALF), cols_last],
            dst_ref=detour_ref.at[step],
            send_sem=detour_send.at[i], recv_sem=detour_recv.at[step],
            device_id={"ctx": ctx(15 if i < 2 else 16), "head": hd}, device_id_type=MESH,
        )

    def forward_copy(i):
        w, slot = detours[i]
        step = i % 3
        return pltpu.make_async_remote_copy(
            src_ref=detour_ref.at[step],
            dst_ref=(kn_ref, vn_ref)[w].at[pl.ds(slot * HALF, HALF), cols_last],
            send_sem=forward_send.at[step], recv_sem=kv_recv.at[w, G - 1, slot],
            device_id={"ctx": ctx(-14), "head": hd}, device_id_type=MESH,
        )

    def relay_copy(w, g, slot, to):
        cols = pl.ds(g * HD, HD)
        near = (kn_ref, vn_ref)[w]
        return pltpu.make_async_remote_copy(
            src_ref=near.at[pl.ds(slot * HALF, HALF), cols],
            dst_ref=near.at[pl.ds(to * HALF, HALF), cols],
            send_sem=relay_send.at[w, g, slot], recv_sem=kv_recv.at[w, g, to],
            device_id={"ctx": ctx(-1), "head": hd}, device_id_type=MESH,
        )

    send_a = [[kv_copy(w, g, 1, 0, 1) for w in range(2)] for g in range(G)]
    send_b = [[kv_copy(w, g, 2, 0, 2) for w in range(2)] for g in range(G)]
    send_far = [[kv_copy(w, g, 3, HALF, 2) for w in range(2)] for g in range(G)]
    relay_low = [[relay_copy(w, g, 2, 1) for w in range(2)] for g in range(G)]
    relay_high = [[relay_copy(w, g, 3, 0) for w in range(2)] for g in range(G)]
    detour = [detour_copy(i) for i in range(5)]
    forward = [forward_copy(i) for i in range(5)]

    def send_blocks():

        @pl.when(c == N_CTX - 1)
        def _():
            for i in (0, 1, 3, 4):
                detour[i].start()

        @pl.when(c == N_CTX - 2)
        def _():
            detour[2].start()

        for g in range(G):
            for copy in send_b[g]:
                copy.start()

            @pl.when(even)
            def _():
                for copy in send_a[g]:
                    copy.start()

            if g == 0:

                @pl.when(c >= N_CTX - 2)
                def _():
                    for copy in send_far[0]:
                        copy.start()

        @pl.when(c == N_CTX - 2)
        def _():
            send_far[1][0].start()

    def pass_on(received, relayed):
        for w in range(2):
            received[w].wait_recv()
            relayed[w].start()

    def wait_all(*groups):
        for group in groups:
            for copy in group:
                copy.wait_recv()

    def relay(g):
        @pl.when((y == 1) & (c != 1))
        def _():
            pass_on(send_b[g], relay_low[g])

    def compact():
        for load in loads[:5]:
            load.wait()
        order = iota((N_CTX, N_CTX), 0)
        lane = iota((N_CTX, TOK), 1).astype(F32)
        for g in range(G):
            match = dest_ref[0, g : g + 1, :] == order
            live = jnp.sum(
                jnp.where(match, count_ref[0, g : g + 1, :].astype(F32), 0.0), 1, keepdims=True
            )
            match = jnp.where(match, 1.0, 0.0).astype(BF)
            rows = rows_ref[0, g]
            high = dot_t(match, (rows >> 4).astype(F32).astype(BF))
            low = dot_t(match, (rows & 15).astype(F32).astype(BF))
            rows = high * 16.0 + low
            pair = jnp.concatenate(
                [k_ref[:, g * HD : (g + 1) * HD], v_ref[:, g * HD : (g + 1) * HD]], 1
            )
            for t in range(KB):
                row = jnp.where(live > t, rows[:, t : t + 1], -1.0)
                pick = jnp.where(row == lane, 1.0, 0.0).astype(BF)
                picked = dot(pick, pair)
                for half in range(2):
                    stage[pl.ds(t * 4 + half * 2 + g, N_CTX, stride=16), :] = picked[
                        :, half * HD : (half + 1) * HD
                    ]
        outgoing[...] = stage[...].reshape(N_CTX, 16, HD).astype(BF)

    def send_block(to):
        @pl.when(to != c)
        def _():
            pltpu.make_async_remote_copy(
                src_ref=outgoing.at[to], dst_ref=cache_ref.at[c],
                send_sem=cache_send, recv_sem=cache_recv,
                device_id={"ctx": to, "head": hd}, device_id_type=MESH,
            ).start()

    def send_layer(there):
        def body(i, carry):
            p = lax.rem(x * 2 + y + i, 8)
            send_block(lax.div(p, 2) * 16 + there * 2 + lax.rem(p, 2))
            return carry

        lax.fori_loop(0, 8, body, 0)

    def send_cache():
        for i in range(8):
            send_layer(lax.rem(z + i, 8))

        cache_ref[c] = outgoing[c]

    mask_l = iota((HALF, 256), 1) <= iota((HALF, 256), 0)
    mask_h = iota((HALF, TOK), 1) <= iota((HALF, TOK), 0) + HALF

    def own_part(g, h, part):
        qs = pl.multiple_of(h * HD, HD)
        low = part == 0
        rs = slice(0, HALF) if low else slice(HALF, TOK)
        n = 256 if low else TOK
        st = {}

        def first():
            s = dot_t(q_ref[rs, pl.ds(qs, HD)], k_ref[:n, g * HD : (g + 1) * HD])
            st["s"] = jnp.where(mask_l if low else mask_h, s, -jnp.inf)
            st["m"] = jnp.max(st["s"], 1, keepdims=True)

        def second():
            w = jnp.exp2((st["s"] - st["m"]) * LOG2E_SCALE).astype(BF)
            (wl if low else wh)[h] = w
            m1[h, rs] = jnp.broadcast_to(st["m"], (HALF, HD))
            ot1[h, rs] = dot(w, with_ones(v_ref[:n, g * HD : (g + 1) * HD]))

        return [first, second]

    def own_attention(g):
        loads[5 + g].wait()

        def own_heads(i, carry):
            units = []
            for u in range(4):
                h = g * QPK + i * 4 + u
                units += [own_part(g, h, 0), own_part(g, h, 1)]
            emit(units, 2)
            return carry

        lax.fori_loop(0, QPK // 4, own_heads, 0)

    compact()

    @pl.when(z == 0)
    def _():
        for g in range(G):
            own_attention(g)

    pl.semaphore_wait(barrier, greeted)
    send_blocks()

    by_way = (c == 14) | (c == 15)

    @pl.when(jnp.logical_not(by_way))
    def _():
        send_cache()

    @pl.when(z != 0)
    def _():
        own_attention(0)

    @pl.when(by_way)
    def _():
        @pl.when(c == 14)
        def _():
            for i in (2, 0, 1):
                detour[i].wait_recv()
                forward[i].start()

        @pl.when(c == 15)
        def _():
            for i in (3, 4):
                detour[i].wait_recv()
                forward[i].start()

        send_cache()

    relay(0)

    @pl.when(z != 0)
    def _():
        own_attention(1)

    relay(1)

    def weights(g, h, rs, start, n, before, unused=0):
        keys = kn_ref[start : start + n, g * HD : (g + 1) * HD]
        s = dot_t(q_ref[rs, pl.ds(pl.multiple_of(h * HD, HD), HD)], keys)
        if unused:
            s = jnp.where(iota(s.shape, 1) >= unused, s, -jnp.inf)
        return s, jnp.maximum(before[h, rs], jnp.max(s, 1, keepdims=True))

    def products(g, s, m, start, n):
        w = jnp.exp2((s - m[:, :1]) * LOG2E_SCALE).astype(BF)
        return w, dot(w, with_ones(vn_ref[start : start + n, g * HD : (g + 1) * HD]))

    def add(acc, i, s):
        if s.shape[1] < TOK:
            s = jnp.concatenate([s, jnp.zeros((8, TOK - s.shape[1]), F32)], 1)
        acc[i] = acc[i] + s

    def middle_part(g, h, rs, start, n, acc, unused=0):
        st = {}

        def first():
            st["s"], st["m"] = weights(g, h, rs, start, n, m1, unused)

        def second():
            w, st["ot"] = products(g, st["s"], st["m"], start, n)
            wm[h, rs, :n] = w

        def third():
            a = jnp.exp2((m1[h, rs] - st["m"]) * LOG2E_SCALE)
            ot1[h, rs] = jnp.concatenate([a, a], 1) * ot1[h, rs] + st["ot"]
            m2[h, rs] = st["m"]

        return [first, second, third]

    def last_part(g, h, rs, start, n, acc, middle=0, unused=0, to=1):
        st = {}
        before = m2 if middle else m1

        def first():
            if n:
                st["s"], st["m"] = weights(g, h, rs, start, n, before, unused)

        def second():
            if n:
                st["w"], st["ot"] = products(g, st["s"], st["m"], start, n)

        def third():
            o1 = ot1[h, rs]
            if n:
                a = jnp.exp2((before[h, rs] - st["m"]) * LOG2E_SCALE)
                inv = 1.0 / (a * o1[:, HD:] + st["ot"][:, HD:])
                o = (a * o1[:, :HD] + st["ot"][:, :HD]) * inv
                f = a * inv
                s = column_sum(st["w"], inv)
                add(acc, to, s[:, :TOK])
                if n > TOK:
                    add(acc, 2, s[:, TOK:])
            else:
                f = 1.0 / o1[:, HD:]
                o = o1[:, :HD] * f
            out_ref[rs, pl.ds(pl.multiple_of(h * HD, HD), HD)] = o.astype(BF)
            if middle:
                add(acc, 2, column_sum(wm[h, rs, :middle], f))
                f = jnp.exp2((m1[h, rs] - m2[h, rs]) * LOG2E_SCALE) * f
            if rs.start < HALF:
                add(acc, 0, column_sum(wl[h], f[:HALF]))
            if rs.stop > HALF:
                add(acc, 0, column_sum(wh[h], f[HALF - rs.start :]))

        return [first, second, third]

    def near_heads(g, parts, carry):
        def heads(i, carry):
            acc = list(carry)
            units = []
            for u in range(UNROLL):
                for part, args in parts:
                    units.append(part(g, g * QPK + i * UNROLL + u, *args[:3], acc, *args[3:]))
            emit(units, 0)
            return tuple(acc)

        return lax.fori_loop(0, QPK // UNROLL, heads, carry)

    def add_up(carry):
        return [jnp.sum(a, 0, keepdims=True) for a in carry]

    whole, low, high = slice(0, TOK), slice(0, HALF), slice(HALF, TOK)
    left = iota((1, TOK), 1) < HALF
    carry = (jnp.zeros((8, TOK), F32),) * 3

    @pl.when(c >= 2)
    def _():
        acc = carry
        for g in range(G):

            @pl.when(even)
            def _():
                wait_all(send_b[g])

            wait_all(send_a[g])
            acc = near_heads(g, [(last_part, (whole, HALF, TOK))], acc)
        own, near, _ = add_up(acc)
        col_send[0] = own
        col_send[1] = jnp.where(left, near, 0.0)
        col_send[2] = pltpu.roll(jnp.where(left, 0.0, near), HALF, 1)

    @pl.when(c == 1)
    def _():
        acc = carry
        start, unused = 2 * HALF - 256, 256 - HALF
        middle = [
            (last_part, (low, start, 256, 0, unused, 2)),
            (middle_part, (high, start, 256, unused)),
        ]
        last = [(last_part, (high, 2 * HALF, TOK, 256))]
        pass_on(send_b[0], relay_low[0])
        wait_all(send_a[0])
        acc = near_heads(0, middle, acc)
        pass_on(send_far[0], relay_high[0])
        wait_all(send_a[1])
        acc = near_heads(1, middle, acc)
        pass_on(send_b[1], relay_low[1])
        acc = near_heads(0, last, acc)
        wait_all(send_far[1])
        acc = near_heads(1, last, acc)
        col_send[0], col_send[2], near = add_up(acc)
        col_send[1] = pltpu.roll(near, TOK - (256 - HALF), 1)

    @pl.when(c == 0)
    def _():
        acc = carry
        for g in range(G):
            acc = near_heads(g, [(last_part, (low, 0, 0))], acc)
        for g in range(G):
            wait_all(send_b[g], send_far[g], send_a[g], relay_high[g])
            acc = near_heads(g, [(last_part, (high, 0, 2 * TOK))], acc)
        own, first, second = add_up(acc)
        first = pltpu.roll(first, HALF, 1)
        col_send[0] = own
        col_send[1] = first
        col_send[2] = second

    sends = []
    for delta in range(3):
        for i in range(4):
            if delta or i:
                sends.append(
                    pltpu.make_async_remote_copy(
                        src_ref=col_send.at[delta], dst_ref=col_recv.at[delta * 4 + i],
                        send_sem=ks_send.at[delta * 4 + i], recv_sem=ks_recv.at[delta * 4 + i],
                        device_id={"ctx": ctx(-delta), "head": head_of(i)}, device_id_type=MESH,
                    )
                )
    for copy in sends:
        copy.start()
    for copy in sends:
        copy.wait_recv()
    total = col_send[0]
    for i in range(1, 12):
        total = total + col_recv[i]
    score_ref[...] = total * (1.0 / QH)

    others = cache_ref.at[pl.ds(0, N_CTX - 1)]
    pltpu.make_async_copy(others, others, cache_recv).wait()
    pltpu.make_async_copy(others, others, cache_send).wait()
    for copy in sends:
        copy.wait_send()
    for g in range(G):
        for copy in send_b[g]:
            copy.wait_send()

        @pl.when(even)
        def _():
            for copy in send_a[g]:
                copy.wait_send()

        @pl.when(odd)
        def _():
            for copy in relay_low[g]:
                copy.wait_send()

    @pl.when(c >= N_CTX - 2)
    def _():
        for copy in send_far[0]:
            copy.wait_send()

    @pl.when(c == N_CTX - 2)
    def _():
        send_far[1][0].wait_send()
        detour[2].wait_send()

    @pl.when(c == N_CTX - 1)
    def _():
        for i in (0, 1, 3, 4):
            detour[i].wait_send()

    @pl.when(c == 14)
    def _():
        for i in (0, 1, 2):
            forward[i].wait_send()

    @pl.when(c == 15)
    def _():
        for i in (3, 4):
            forward[i].wait_send()

    @pl.when(c == 1)
    def _():
        for copy in relay_high[0]:
            copy.wait_send()


def tail(a_in, s_in, c_in, a_out, s_out, c_out, sem):
    copies = [
        pltpu.make_async_copy(a_in, a_out, sem.at[0]),
        pltpu.make_async_copy(c_in, c_out, sem.at[1]),
        pltpu.make_async_copy(s_in.at[0], s_out, sem.at[2]),
    ]
    for copy in copies:
        copy.start()
    for copy in copies:
        copy.wait()


def on_device(queries, keys, values, keep_rows, keep_dest, keep_count):
    dma = pltpu.SemaphoreType.DMA
    anywhere = pl.BlockSpec(memory_space=pl.ANY)
    operands = [queries, keys, values, keep_rows.transpose(0, 1, 3, 2), keep_dest, keep_count]
    results = pl.pallas_call(
        lambda *refs: kernel(*refs),
        name="window",
        out_shape=[
            jax.ShapeDtypeStruct((TOK, HEADS * HD), BF),
            jax.ShapeDtypeStruct((1, TOK), F32),
            jax.ShapeDtypeStruct((N_CTX, 16, HD), BF),
        ],
        in_specs=[anywhere] * 6,
        out_specs=[pl.BlockSpec(memory_space=pltpu.VMEM)] * 3,
        scratch_shapes=[
            pltpu.VMEM((TOK, HEADS * HD), BF),
            pltpu.VMEM((TOK, G * HD), BF),
            pltpu.VMEM((TOK, G * HD), BF),
            pltpu.VMEM((1, G, KB, N_CTX), jnp.int32),
            pltpu.VMEM((1, G, N_CTX), jnp.int32),
            pltpu.VMEM((1, G, N_CTX), jnp.int32),
            pltpu.VMEM((4 * HALF, G * HD), BF),
            pltpu.VMEM((4 * HALF, G * HD), BF),
            pltpu.VMEM((3, HALF, HD), BF),
            pltpu.VMEM((N_CTX * 16, HD), F32),
            pltpu.VMEM((N_CTX, 16, HD), BF),
            pltpu.VMEM((HEADS, TOK, 2 * HD), F32),
            pltpu.VMEM((HEADS, TOK, HD), F32),
            pltpu.VMEM((HEADS, TOK, HD), F32),
            pltpu.VMEM((HEADS, HALF, 256), BF),
            pltpu.VMEM((HEADS, HALF, TOK), BF),
            pltpu.VMEM((HEADS, TOK, 256), BF),
            pltpu.VMEM((3, 1, TOK), F32),
            pltpu.VMEM((12, 1, TOK), F32),
            dma((7,)), dma, dma,
            dma((2, G, 4)), dma((2, G, 4)), dma((2, G, 4)), dma((5,)), dma((3,)), dma((3,)),
            dma((12,)), dma((12,)),
        ],
        compiler_params=pltpu.CompilerParams(
            collective_id=0, has_side_effects=True, vmem_limit_bytes=40 << 20
        ),
        cost_estimate=pl.CostEstimate(
            flops=2_200_000_000, bytes_accessed=4_000_000, transcendentals=4_200_000
        ),
    )(*[pltpu.with_memory_space_constraint(v, pltpu.HBM) for v in operands])
    attended, scores, cache = pl.pallas_call(
        tail,
        name="tail",
        out_shape=[
            jax.ShapeDtypeStruct((TOK, HEADS * HD), BF),
            jax.ShapeDtypeStruct((TOK,), F32),
            jax.ShapeDtypeStruct((N_CTX, 16, HD), BF),
        ],
        in_specs=[anywhere] * 3,
        out_specs=[anywhere] * 3,
        scratch_shapes=[dma((3,))],
        compiler_params=pltpu.CompilerParams(vmem_limit_bytes=1 << 20),
    )(*results)
    cache = cache.reshape(N_CTX, KB, 2, G, HD).transpose(0, 1, 3, 2, 4)
    return attended, scores, cache.reshape(1, N_CTX, KB, G, 2 * HD)


def solution(mesh):
    return jax.shard_map(
        on_device,
        mesh=mesh,
        in_specs=(
            P("ctx", "head"),
            P("ctx", "head"),
            P("ctx", "head"),
            P("ctx", "head", None, None),
            P("ctx", "head", None),
            P("ctx", "head", None),
        ),
        out_specs=(P("ctx", "head"), P("ctx"), P("ctx", None, None, "head", None)),
        check_vma=False,
    )
```

```python
import jax
import jax.numpy as jnp
from jax import lax
from jax.experimental import pallas as pl
from jax.experimental.pallas import tpu as pltpu
from jax.sharding import PartitionSpec as P

HD = 128
KB = 4
QH = 64
TOK = 384
HALF = 192
G = 2
QPK = 8
HEADS = G * QPK
N_CTX = 64
F32 = jnp.float32
BF = jnp.bfloat16
LOG2E_SCALE = HD**-0.5 * 1.4426950408889634
MESH = pl.DeviceIdType.MESH
UNROLL = 8


def dot(a, b):
    return lax.dot_general(a, b, (((1,), (0,)), ((), ())), preferred_element_type=F32)


def dot_t(a, b):
    return lax.dot_general(a, b, (((1,), (1,)), ((), ())), preferred_element_type=F32)


def iota(shape, dim):
    return lax.broadcasted_iota(jnp.int32, shape, dim)


def with_ones(v):
    return jnp.concatenate([v, jnp.ones(v.shape, BF)], 1)


def column_sum(w, f):
    r, n = w.shape
    return jnp.sum((w.astype(F32) * f[:, :1]).reshape(r // 8, 8, n), 0)


def emit(units, skew):
    stages = max(len(u) for u in units)
    for t in range(len(units) + (stages - 1) * skew):
        for k in range(stages):
            i = t - k * skew
            if 0 <= i < len(units) and k < len(units[i]):
                units[i][k]()


def kernel(
    q_hbm, k_hbm, v_hbm, rows_hbm, dest_hbm, count_hbm,
    out_ref, score_ref, cache_ref,
    q_ref, k_ref, v_ref, rows_ref, dest_ref, count_ref,
    kn_ref, vn_ref, detour_ref, stage, outgoing,
    ot1, m1, m2, wl, wh, wm, col_send, col_recv,
    in_sem, cache_send, cache_recv, kv_send, kv_recv, relay_send, detour_send, detour_recv, forward_send,
    ks_send, ks_recv,
):
    c = lax.axis_index("ctx")
    hd = lax.axis_index("head")
    x = lax.div(c, 16)
    z = lax.rem(lax.div(c, 2), 8)
    y = lax.rem(c, 2)
    odd = y == 1
    even = y == 0

    def ctx(delta):
        return lax.rem(c + delta + N_CTX, N_CTX)

    def head_of(i):
        return lax.rem(hd + i, 4)

    barrier = pltpu.get_barrier_semaphore()
    def greet(a, b):
        pl.semaphore_signal(barrier, inc=1, device_id={"ctx": a, "head": b}, device_id_type=MESH)

    def greet_row(i, carry):
        greet(ctx(i), hd)
        return carry

    lax.fori_loop(1, N_CTX, greet_row, 0)
    greeted = N_CTX - 1
    for delta in range(3):
        for i in range(1, 4):
            greet(ctx(delta), head_of(i))
            greeted += 1

    @pl.when(c == 1)
    def _():
        kn_ref[2 * HALF - 256 : HALF, :] = jnp.zeros((256 - HALF, G * HD), BF)
        vn_ref[2 * HALF - 256 : HALF, :] = jnp.zeros((256 - HALF, G * HD), BF)

    loads = [
        pltpu.make_async_copy(src, dst, in_sem.at[i])
        for i, (src, dst) in enumerate(
            [
                (k_hbm, k_ref), (v_hbm, v_ref), (rows_hbm, rows_ref), (dest_hbm, dest_ref),
                (count_hbm, count_ref),
                (q_hbm.at[:, pl.ds(0, QPK * HD)], q_ref.at[:, pl.ds(0, QPK * HD)]),
                (q_hbm.at[:, pl.ds(QPK * HD, QPK * HD)], q_ref.at[:, pl.ds(QPK * HD, QPK * HD)]),
            ]
        )
    ]
    for load in loads:
        load.start()

    def kv_copy(w, g, slot, row, delta):
        cols = pl.ds(g * HD, HD)
        return pltpu.make_async_remote_copy(
            src_ref=(k_hbm, v_hbm)[w].at[pl.ds(row, HALF), cols],
            dst_ref=(kn_ref, vn_ref)[w].at[pl.ds(slot * HALF, HALF), cols],
            send_sem=kv_send.at[w, g, slot], recv_sem=kv_recv.at[w, g, slot],
            device_id={"ctx": ctx(delta), "head": hd}, device_id_type=MESH,
        )

    detours = [(0, 0), (1, 0), (1, 3), (0, 3), (1, 3)]
    cols_last = pl.ds((G - 1) * HD, HD)

    def detour_copy(i):
        w, slot = detours[i]
        step = i % 3
        return pltpu.make_async_remote_copy(
            src_ref=(k_hbm, v_hbm)[w].at[pl.ds(HALF, HALF), cols_last],
            dst_ref=detour_ref.at[step],
            send_sem=detour_send.at[i], recv_sem=detour_recv.at[step],
            device_id={"ctx": ctx(15 if i < 2 else 16), "head": hd}, device_id_type=MESH,
        )

    def forward_copy(i):
        w, slot = detours[i]
        step = i % 3
        return pltpu.make_async_remote_copy(
            src_ref=detour_ref.at[step],
            dst_ref=(kn_ref, vn_ref)[w].at[pl.ds(slot * HALF, HALF), cols_last],
            send_sem=forward_send.at[step], recv_sem=kv_recv.at[w, G - 1, slot],
            device_id={"ctx": ctx(-14), "head": hd}, device_id_type=MESH,
        )

    def relay_copy(w, g, slot, to):
        cols = pl.ds(g * HD, HD)
        near = (kn_ref, vn_ref)[w]
        return pltpu.make_async_remote_copy(
            src_ref=near.at[pl.ds(slot * HALF, HALF), cols],
            dst_ref=near.at[pl.ds(to * HALF, HALF), cols],
            send_sem=relay_send.at[w, g, slot], recv_sem=kv_recv.at[w, g, to],
            device_id={"ctx": ctx(-1), "head": hd}, device_id_type=MESH,
        )

    send_a = [[kv_copy(w, g, 1, 0, 1) for w in range(2)] for g in range(G)]
    send_b = [[kv_copy(w, g, 2, 0, 2) for w in range(2)] for g in range(G)]
    send_far = [[kv_copy(w, g, 3, HALF, 2) for w in range(2)] for g in range(G)]
    relay_low = [[relay_copy(w, g, 2, 1) for w in range(2)] for g in range(G)]
    relay_high = [[relay_copy(w, g, 3, 0) for w in range(2)] for g in range(G)]
    detour = [detour_copy(i) for i in range(5)]
    forward = [forward_copy(i) for i in range(5)]

    def send_blocks():

        @pl.when(c == N_CTX - 1)
        def _():
            for i in (0, 1, 3, 4):
                detour[i].start()

        @pl.when(c == N_CTX - 2)
        def _():
            detour[2].start()

        for g in range(G):
            for copy in send_b[g]:
                copy.start()

            @pl.when(even)
            def _():
                for copy in send_a[g]:
                    copy.start()

            if g == 0:

                @pl.when(c >= N_CTX - 2)
                def _():
                    for copy in send_far[0]:
                        copy.start()

        @pl.when(c == N_CTX - 2)
        def _():
            send_far[1][0].start()

    def pass_on(received, relayed):
        for w in range(2):
            received[w].wait_recv()
            relayed[w].start()

    def wait_all(*groups):
        for group in groups:
            for copy in group:
                copy.wait_recv()

    def relay(g):
        @pl.when((y == 1) & (c != 1))
        def _():
            pass_on(send_b[g], relay_low[g])

    def compact():
        for load in loads[:5]:
            load.wait()
        order = iota((N_CTX, N_CTX), 0)
        lane = iota((N_CTX, TOK), 1).astype(F32)
        for g in range(G):
            match = dest_ref[0, g : g + 1, :] == order
            live = jnp.sum(
                jnp.where(match, count_ref[0, g : g + 1, :].astype(F32), 0.0), 1, keepdims=True
            )
            match = jnp.where(match, 1.0, 0.0).astype(BF)
            rows = rows_ref[0, g]
            high = dot_t(match, (rows >> 4).astype(F32).astype(BF))
            low = dot_t(match, (rows & 15).astype(F32).astype(BF))
            rows = high * 16.0 + low
            pair = jnp.concatenate(
                [k_ref[:, g * HD : (g + 1) * HD], v_ref[:, g * HD : (g + 1) * HD]], 1
            )
            for t in range(KB):
                row = jnp.where(live > t, rows[:, t : t + 1], -1.0)
                pick = jnp.where(row == lane, 1.0, 0.0).astype(BF)
                picked = dot(pick, pair)
                for half in range(2):
                    stage[pl.ds(t * 4 + half * 2 + g, N_CTX, stride=16), :] = picked[
                        :, half * HD : (half + 1) * HD
                    ]
        outgoing[...] = stage[...].reshape(N_CTX, 16, HD).astype(BF)

    def send_block(to):
        @pl.when(to != c)
        def _():
            pltpu.make_async_remote_copy(
                src_ref=outgoing.at[to], dst_ref=cache_ref.at[c],
                send_sem=cache_send, recv_sem=cache_recv,
                device_id={"ctx": to, "head": hd}, device_id_type=MESH,
            ).start()

    def send_layer(there):
        def body(i, carry):
            p = lax.rem(x * 2 + y + i, 8)
            send_block(lax.div(p, 2) * 16 + there * 2 + lax.rem(p, 2))
            return carry

        lax.fori_loop(0, 8, body, 0)

    def send_cache():
        for i in range(8):
            send_layer(lax.rem(z + i, 8))

        cache_ref[c] = outgoing[c]

    mask_l = iota((HALF, 256), 1) <= iota((HALF, 256), 0)
    mask_h = iota((HALF, TOK), 1) <= iota((HALF, TOK), 0) + HALF

    def own_part(g, h, part):
        qs = pl.multiple_of(h * HD, HD)
        low = part == 0
        rs = slice(0, HALF) if low else slice(HALF, TOK)
        n = 256 if low else TOK
        st = {}

        def first():
            s = dot_t(q_ref[rs, pl.ds(qs, HD)], k_ref[:n, g * HD : (g + 1) * HD])
            st["s"] = jnp.where(mask_l if low else mask_h, s, -jnp.inf)
            st["m"] = jnp.max(st["s"], 1, keepdims=True)

        def second():
            w = jnp.exp2((st["s"] - st["m"]) * LOG2E_SCALE).astype(BF)
            (wl if low else wh)[h] = w
            m1[h, rs] = jnp.broadcast_to(st["m"], (HALF, HD))
            ot1[h, rs] = dot(w, with_ones(v_ref[:n, g * HD : (g + 1) * HD]))

        return [first, second]

    def own_attention(g):
        loads[5 + g].wait()

        def own_heads(i, carry):
            units = []
            for u in range(4):
                h = g * QPK + i * 4 + u
                units += [own_part(g, h, 0), own_part(g, h, 1)]
            emit(units, 2)
            return carry

        lax.fori_loop(0, QPK // 4, own_heads, 0)

    compact()

    @pl.when(z == 0)
    def _():
        for g in range(G):
            own_attention(g)

    pl.semaphore_wait(barrier, greeted)
    send_blocks()

    by_way = (c == 14) | (c == 15)

    @pl.when(jnp.logical_not(by_way))
    def _():
        send_cache()

    @pl.when(z != 0)
    def _():
        own_attention(0)

    @pl.when(by_way)
    def _():
        @pl.when(c == 14)
        def _():
            for i in (2, 0, 1):
                detour[i].wait_recv()
                forward[i].start()

        @pl.when(c == 15)
        def _():
            for i in (3, 4):
                detour[i].wait_recv()
                forward[i].start()

        send_cache()

    relay(0)

    @pl.when(z != 0)
    def _():
        own_attention(1)

    relay(1)

    def weights(g, h, rs, start, n, before, unused=0):
        keys = kn_ref[start : start + n, g * HD : (g + 1) * HD]
        s = dot_t(q_ref[rs, pl.ds(pl.multiple_of(h * HD, HD), HD)], keys)
        if unused:
            s = jnp.where(iota(s.shape, 1) >= unused, s, -jnp.inf)
        return s, jnp.maximum(before[h, rs], jnp.max(s, 1, keepdims=True))

    def products(g, s, m, start, n):
        w = jnp.exp2((s - m[:, :1]) * LOG2E_SCALE).astype(BF)
        return w, dot(w, with_ones(vn_ref[start : start + n, g * HD : (g + 1) * HD]))

    def add(acc, i, s):
        if s.shape[1] < TOK:
            s = jnp.concatenate([s, jnp.zeros((8, TOK - s.shape[1]), F32)], 1)
        acc[i] = acc[i] + s

    def middle_part(g, h, rs, start, n, acc, unused=0):
        st = {}

        def first():
            st["s"], st["m"] = weights(g, h, rs, start, n, m1, unused)

        def second():
            w, st["ot"] = products(g, st["s"], st["m"], start, n)
            wm[h, rs, :n] = w

        def third():
            a = jnp.exp2((m1[h, rs] - st["m"]) * LOG2E_SCALE)
            ot1[h, rs] = jnp.concatenate([a, a], 1) * ot1[h, rs] + st["ot"]
            m2[h, rs] = st["m"]

        return [first, second, third]

    def last_part(g, h, rs, start, n, acc, middle=0, unused=0, to=1):
        st = {}
        before = m2 if middle else m1

        def first():
            if n:
                st["s"], st["m"] = weights(g, h, rs, start, n, before, unused)

        def second():
            if n:
                st["w"], st["ot"] = products(g, st["s"], st["m"], start, n)

        def third():
            o1 = ot1[h, rs]
            if n:
                a = jnp.exp2((before[h, rs] - st["m"]) * LOG2E_SCALE)
                inv = 1.0 / (a * o1[:, HD:] + st["ot"][:, HD:])
                o = (a * o1[:, :HD] + st["ot"][:, :HD]) * inv
                f = a * inv
                s = column_sum(st["w"], inv)
                add(acc, to, s[:, :TOK])
                if n > TOK:
                    add(acc, 2, s[:, TOK:])
            else:
                f = 1.0 / o1[:, HD:]
                o = o1[:, :HD] * f
            out_ref[rs, pl.ds(pl.multiple_of(h * HD, HD), HD)] = o.astype(BF)
            if middle:
                add(acc, 2, column_sum(wm[h, rs, :middle], f))
                f = jnp.exp2((m1[h, rs] - m2[h, rs]) * LOG2E_SCALE) * f
            if rs.start < HALF:
                add(acc, 0, column_sum(wl[h], f[:HALF]))
            if rs.stop > HALF:
                add(acc, 0, column_sum(wh[h], f[HALF - rs.start :]))

        return [first, second, third]

    def near_heads(g, parts, carry):
        def heads(i, carry):
            acc = list(carry)
            units = []
            for u in range(UNROLL):
                for part, args in parts:
                    units.append(part(g, g * QPK + i * UNROLL + u, *args[:3], acc, *args[3:]))
            emit(units, 0)
            return tuple(acc)

        return lax.fori_loop(0, QPK // UNROLL, heads, carry)

    def add_up(carry):
        return [jnp.sum(a, 0, keepdims=True) for a in carry]

    whole, low, high = slice(0, TOK), slice(0, HALF), slice(HALF, TOK)
    left = iota((1, TOK), 1) < HALF
    carry = (jnp.zeros((8, TOK), F32),) * 3

    @pl.when(c >= 2)
    def _():
        acc = carry
        for g in range(G):

            @pl.when(even)
            def _():
                wait_all(send_b[g])

            wait_all(send_a[g])
            acc = near_heads(g, [(last_part, (whole, HALF, TOK))], acc)
        own, near, _ = add_up(acc)
        col_send[0] = own
        col_send[1] = jnp.where(left, near, 0.0)
        col_send[2] = pltpu.roll(jnp.where(left, 0.0, near), HALF, 1)

    @pl.when(c == 1)
    def _():
        acc = carry
        start, unused = 2 * HALF - 256, 256 - HALF
        middle = [
            (last_part, (low, start, 256, 0, unused, 2)),
            (middle_part, (high, start, 256, unused)),
        ]
        last = [(last_part, (high, 2 * HALF, TOK, 256))]
        pass_on(send_b[0], relay_low[0])
        wait_all(send_a[0])
        acc = near_heads(0, middle, acc)
        pass_on(send_far[0], relay_high[0])
        wait_all(send_a[1])
        acc = near_heads(1, middle, acc)
        pass_on(send_b[1], relay_low[1])
        acc = near_heads(0, last, acc)
        wait_all(send_far[1])
        acc = near_heads(1, last, acc)
        col_send[0], col_send[2], near = add_up(acc)
        col_send[1] = pltpu.roll(near, TOK - (256 - HALF), 1)

    @pl.when(c == 0)
    def _():
        acc = carry
        for g in range(G):
            acc = near_heads(g, [(last_part, (low, 0, 0))], acc)
        for g in range(G):
            wait_all(send_b[g], send_far[g], send_a[g], relay_high[g])
            acc = near_heads(g, [(last_part, (high, 0, 2 * TOK))], acc)
        own, first, second = add_up(acc)
        first = pltpu.roll(first, HALF, 1)
        col_send[0] = own
        col_send[1] = first
        col_send[2] = second

    sends = []
    for delta in (2, 1, 0):
        for i in range(4):
            if delta or i:
                sends.append(
                    pltpu.make_async_remote_copy(
                        src_ref=col_send.at[delta], dst_ref=col_recv.at[delta * 4 + i],
                        send_sem=ks_send.at[delta * 4 + i], recv_sem=ks_recv.at[delta * 4 + i],
                        device_id={"ctx": ctx(-delta), "head": head_of(i)}, device_id_type=MESH,
                    )
                )
    for copy in sends:
        copy.start()
    for copy in sends:
        copy.wait_recv()
    total = col_send[0]
    for i in range(1, 12):
        total = total + col_recv[i]
    score_ref[...] = total * (1.0 / QH)

    others = cache_ref.at[pl.ds(0, N_CTX - 1)]
    pltpu.make_async_copy(others, others, cache_recv).wait()
    pltpu.make_async_copy(others, others, cache_send).wait()
    for copy in sends:
        copy.wait_send()
    for g in range(G):
        for copy in send_b[g]:
            copy.wait_send()

        @pl.when(even)
        def _():
            for copy in send_a[g]:
                copy.wait_send()

        @pl.when(odd)
        def _():
            for copy in relay_low[g]:
                copy.wait_send()

    @pl.when(c >= N_CTX - 2)
    def _():
        for copy in send_far[0]:
            copy.wait_send()

    @pl.when(c == N_CTX - 2)
    def _():
        send_far[1][0].wait_send()
        detour[2].wait_send()

    @pl.when(c == N_CTX - 1)
    def _():
        for i in (0, 1, 3, 4):
            detour[i].wait_send()

    @pl.when(c == 14)
    def _():
        for i in (0, 1, 2):
            forward[i].wait_send()

    @pl.when(c == 15)
    def _():
        for i in (3, 4):
            forward[i].wait_send()

    @pl.when(c == 1)
    def _():
        for copy in relay_high[0]:
            copy.wait_send()


def tail(a_in, s_in, c_in, a_out, s_out, c_out, sem):
    copies = [
        pltpu.make_async_copy(s_in.at[0], s_out, sem.at[0]),
        pltpu.make_async_copy(c_in, c_out, sem.at[1]),
    ]
    for i in range(4):
        rows = pl.ds(i * (TOK // 4), TOK // 4)
        copies.append(pltpu.make_async_copy(a_in.at[rows], a_out.at[rows], sem.at[2 + i]))
    for copy in copies:
        copy.start()
    for copy in copies:
        copy.wait()


def on_device(queries, keys, values, keep_rows, keep_dest, keep_count):
    dma = pltpu.SemaphoreType.DMA
    anywhere = pl.BlockSpec(memory_space=pl.ANY)
    operands = [queries, keys, values, keep_rows.transpose(0, 1, 3, 2), keep_dest, keep_count]
    results = pl.pallas_call(
        lambda *refs: kernel(*refs),
        name="window",
        out_shape=[
            jax.ShapeDtypeStruct((TOK, HEADS * HD), BF),
            jax.ShapeDtypeStruct((1, TOK), F32),
            jax.ShapeDtypeStruct((N_CTX, 16, HD), BF),
        ],
        in_specs=[anywhere] * 6,
        out_specs=[pl.BlockSpec(memory_space=pltpu.VMEM)] * 3,
        scratch_shapes=[
            pltpu.VMEM((TOK, HEADS * HD), BF),
            pltpu.VMEM((TOK, G * HD), BF),
            pltpu.VMEM((TOK, G * HD), BF),
            pltpu.VMEM((1, G, KB, N_CTX), jnp.int32),
            pltpu.VMEM((1, G, N_CTX), jnp.int32),
            pltpu.VMEM((1, G, N_CTX), jnp.int32),
            pltpu.VMEM((4 * HALF, G * HD), BF),
            pltpu.VMEM((4 * HALF, G * HD), BF),
            pltpu.VMEM((3, HALF, HD), BF),
            pltpu.VMEM((N_CTX * 16, HD), F32),
            pltpu.VMEM((N_CTX, 16, HD), BF),
            pltpu.VMEM((HEADS, TOK, 2 * HD), F32),
            pltpu.VMEM((HEADS, TOK, HD), F32),
            pltpu.VMEM((HEADS, TOK, HD), F32),
            pltpu.VMEM((HEADS, HALF, 256), BF),
            pltpu.VMEM((HEADS, HALF, TOK), BF),
            pltpu.VMEM((HEADS, TOK, 256), BF),
            pltpu.VMEM((3, 1, TOK), F32),
            pltpu.VMEM((12, 1, TOK), F32),
            dma((7,)), dma, dma,
            dma((2, G, 4)), dma((2, G, 4)), dma((2, G, 4)), dma((5,)), dma((3,)), dma((3,)),
            dma((12,)), dma((12,)),
        ],
        compiler_params=pltpu.CompilerParams(
            collective_id=0, has_side_effects=True, vmem_limit_bytes=40 << 20
        ),
        cost_estimate=pl.CostEstimate(
            flops=2_200_000_000, bytes_accessed=4_000_000, transcendentals=4_200_000
        ),
    )(*[pltpu.with_memory_space_constraint(v, pltpu.HBM) for v in operands])
    attended, scores, cache = pl.pallas_call(
        tail,
        name="tail",
        out_shape=[
            jax.ShapeDtypeStruct((TOK, HEADS * HD), BF),
            jax.ShapeDtypeStruct((TOK,), F32),
            jax.ShapeDtypeStruct((N_CTX, 16, HD), BF),
        ],
        in_specs=[anywhere] * 3,
        out_specs=[anywhere] * 3,
        scratch_shapes=[dma((6,))],
        compiler_params=pltpu.CompilerParams(vmem_limit_bytes=1 << 20),
    )(*results)
    cache = cache.reshape(N_CTX, KB, 2, G, HD).transpose(0, 1, 3, 2, 4)
    return attended, scores, cache.reshape(1, N_CTX, KB, G, 2 * HD)


def solution(mesh):
    return jax.shard_map(
        on_device,
        mesh=mesh,
        in_specs=(
            P("ctx", "head"),
            P("ctx", "head"),
            P("ctx", "head"),
            P("ctx", "head", None, None),
            P("ctx", "head", None),
            P("ctx", "head", None),
        ),
        out_specs=(P("ctx", "head"), P("ctx"), P("ctx", None, None, "head", None)),
        check_vma=False,
    )
```
